512 devices in a mesh: dp: 32 (over x, z_hi, core), tensor: 16 (over y, z_lo).
Axes of the slice: x: 4, y: 4, z: 16 (z_hi: 4, z_lo: 4; z = z_hi * 4 + z_lo), core: 2. Of those that a mesh axis runs over, the one named last changes fastest.
Arguments:
- tokens: bfloat16 [4096, 4096], P('dp', 'tensor'), may hold values from -6 to 6
- weight: bfloat16 [4096, 14336], P('dp', 'tensor'), may hold values from -0.09375 to 0.09375
- cotangent: bfloat16 [4096, 14336], P('dp', 'tensor'), may hold values from -6 to 6
- levels: int32 [28], replicated, may hold values from 0 to 8
Outputs:
- output: bfloat16 [4096, 14336], P('dp', 'tensor')
- input_grad: bfloat16 [4096, 4096], P('dp', 'tensor')
- weight_grad: float32 [4096, 14336], P('dp', 'tensor')
The draws below stay inside these ranges and needn't reach their ends.
All inputs are finite; a program needn't handle non-finite values.
Results may differ from the reference program's by a relative error of at most 0.022.
Values may be sent and summed in bfloat16 or wider, within the bound.
No kernel may reach another device: no remote copies, remote signals or barrier semaphores. Data moves between devices by JAX's collectives and lax.ppermute only.
A program may use at most 128 MiB of HBM per device.

```python
import jax
import jax.numpy as jnp
from jax import lax

D = 4096
F = 14336
BLOCK = 512
TOK_DEV = 128
TOKENS = 4096
BLOCKS = 28
N_DP = 32
N_TENSOR = 16


def place_ends(drawn, stream_key, smallest, top_value):
    shape = drawn.shape
    index_at = [jax.random.randint(jax.random.fold_in(stream_key, axis), (), 0, shape[axis]) for axis in range(len(shape))]
    drawn = drawn.at[tuple(index_at)].set(smallest)
    longest = shape.index(max(shape))
    index_at[longest] = (index_at[longest] + 1) % shape[longest]
    return drawn.at[tuple(index_at)].set(top_value)


def spiked(array, key, source, target, shards_of, factor):
    owner, partner = [(jnp.arange(array.shape[axis_at]) // (array.shape[axis_at] // shards_of)).reshape([-1 if axis == axis_at else 1 for axis in range(array.ndim)]) for axis_at in (source, target)]
    chosen = jax.random.permutation(key, shards_of)[partner]
    strong = (owner == chosen) | (owner == (partner + shards_of // 2) % shards_of)
    return jnp.where(strong, factor * array, array)


def block_scale(key, dims, cuts, low, top_value):
    loudness, own = 1.0, jax.random.fold_in(key, 6)
    for dim, blocks in cuts:
        steps = jnp.exp(jax.random.uniform(jax.random.fold_in(own, dim), (blocks,), jnp.float32, low / len(cuts), top_value / len(cuts)))
        loudness = loudness * jnp.repeat(steps, dims[dim] // blocks).reshape([-1 if axis == dim else 1 for axis in range(len(dims))])
    return loudness


def normal_values(rng, extent, spread, reach, cuts=(), held_as=jnp.bfloat16):
    array = jax.random.normal(rng, extent, jnp.float32) * spread
    if len(cuts) > 0:
        array = block_scale(rng, extent, cuts, -0.22, 0.18) * array
    return jnp.clip(array, min=-reach, max=reach).astype(held_as)


def bell_draw_with(own_key, dims, scale, bound, split, heavy, held_as=jnp.bfloat16):
    array = scale * jax.random.normal(own_key, dims, jnp.float32)
    if split:
        array = array * block_scale(own_key, dims, split, -0.22, 0.18)
    return jnp.clip(spiked(array, jax.random.fold_in(own_key, 3), *heavy), -bound, bound).astype(held_as)


def setup_inputs(seed: int = 0) -> dict:
    seeds = jax.random.split(jax.random.key(seed), 5)
    return {
        "tokens": bell_draw_with(seeds[0], (TOKENS, D), 1.0, 6.0, ((0, 32), (1, 16)), (0, 1, 32, 2.75)),
        "weight": normal_values(seeds[1], (D, F), D ** -0.5, 0.09375, ((0, 32), (1, 16))),
        "cotangent": normal_values(seeds[2], (TOKENS, F), 1.0, 6.0, ((0, 32), (1, 16))),
        "levels": place_ends(jax.random.randint(seeds[3], (BLOCKS,), 0, 9), jax.random.fold_in(seeds[3], 1), 0, 8).astype(jnp.int32),
    }


def reference(tokens, weight, cotangent, levels):
    col_scale = jnp.repeat(levels.astype(jnp.float32) / 8.0, BLOCK)
    output = (jnp.dot(tokens, weight, preferred_element_type=jnp.float32) * col_scale).astype(jnp.bfloat16)
    scaled = (cotangent.astype(jnp.float32) * col_scale).astype(jnp.bfloat16)
    group_width = F // N_TENSOR

    def column_group(running, group_id):
        begin = (group_id * group_width).astype(jnp.int32)
        part_cot = lax.dynamic_slice_in_dim(scaled, begin, group_width, 1)
        part_weight = lax.dynamic_slice_in_dim(weight, begin, group_width, 1)
        partial_value = jnp.dot(part_cot, part_weight.T, preferred_element_type=jnp.float32).astype(jnp.bfloat16)
        partial_value = lax.optimization_barrier(partial_value)
        return (running + partial_value.astype(jnp.float32), None)
    input_total, _ = lax.scan(column_group, jnp.zeros((TOKENS, D), jnp.float32), jnp.arange(N_TENSOR, dtype=jnp.int32))
    input_grad = input_total.astype(jnp.bfloat16)

    def token_group(running, group_id):
        begin = (group_id * TOK_DEV).astype(jnp.int32)
        part_tok = lax.dynamic_slice_in_dim(tokens, begin, TOK_DEV, 0)
        part_cot = lax.dynamic_slice_in_dim(scaled, begin, TOK_DEV, 0)
        partial_value = jnp.dot(part_tok.T, part_cot, preferred_element_type=jnp.float32).astype(jnp.bfloat16)
        partial_value = lax.optimization_barrier(partial_value)
        return (running + partial_value.astype(jnp.float32), None)
    grad_total, _ = lax.scan(token_group, jnp.zeros((D, F), jnp.float32), jnp.arange(N_DP, dtype=jnp.int32))
    weight_grad = grad_total * (1.0 / jnp.sqrt(jnp.float32(TOKENS)))
    return (output, input_grad, weight_grad)
```

```python
import jax
import jax.numpy as jnp
from jax import lax
from jax.sharding import PartitionSpec as P

BLOCK = 512
RING = 4
PARTS = 32
GROUPS = 16


def dp_of(x, z, core):
    return ((x % RING) * RING + z % RING) * 2 + core


def dp_pairs(dx, dz, flip):
    return [
        (dp_of(x + dx, z + dz, core ^ flip), dp_of(x, z, core))
        for x in range(RING)
        for z in range(RING)
        for core in range(2)
    ]


def tensor_pairs(dy, dz):
    return [
        (((y + dy) % RING) * RING + (z + dz) % RING, y * RING + z)
        for y in range(RING)
        for z in range(RING)
    ]


def swap_pairs():
    return [
        ((chip * 2 + core) * GROUPS + group, (group * 2 + core) * GROUPS + chip)
        for chip in range(GROUPS)
        for core in range(2)
        for group in range(GROUPS)
    ]


def from_x(block, shift):
    return lax.ppermute(block, "dp", dp_pairs(shift, 0, 0))


def from_z(block, shift):
    return lax.ppermute(block, "dp", dp_pairs(0, shift, 0))


def from_core(block):
    return lax.ppermute(block, "dp", dp_pairs(0, 0, 1))


def ring(block, fetch, forward):
    ahead = fetch(block, 1)
    behind = fetch(block, -1)
    far = fetch(ahead, 1) if forward > 0 else fetch(behind, -1)
    return block, ahead, far, behind


def gather_pairwise(block, forward):
    own, ahead, far, behind = ring(block, from_z, forward)
    own_x = ring(own, from_x, forward)
    sides_x = ring(jnp.stack([ahead, behind]), from_x, -forward)
    far_x = ring(far, from_x, forward)
    rows = []
    for i in range(RING):
        rows += [own_x[i], sides_x[i][0], far_x[i], sides_x[i][1]]
    return jnp.concatenate(rows, axis=0)


def rolled(array, start):
    return lax.dynamic_slice_in_dim(jnp.concatenate([array, array], axis=0), start, array.shape[0], 0)


def on_device(tokens, weight, cotangent, levels):
    token_rows = tokens.shape[0]
    local_cols = weight.shape[1]
    dp_count = lax.axis_size("dp")
    dp = lax.axis_index("dp")
    tensor = lax.axis_index("tensor")
    core = dp % 2
    x, z_hi = dp // (2 * RING), (dp // 2) % RING
    y, z_lo = tensor // RING, tensor % RING
    half = tokens.shape[1] // 2

    col_start = tensor * local_cols
    column_ids = col_start + jnp.arange(local_cols, dtype=jnp.int32)
    block_ids = column_ids // BLOCK
    block_range = jnp.arange(levels.shape[0], dtype=jnp.int32)
    membership = (block_ids[None, :] == block_range[:, None]).astype(jnp.float32)
    level_vals = levels.astype(jnp.float32) / 8.0
    col_scale = jnp.sum(membership * level_vals[:, None], axis=0)
    scaled = (cotangent.astype(jnp.float32) * col_scale[None, :]).astype(jnp.bfloat16)

    weight_all = gather_pairwise(weight, 1)

    halves = tokens.T.reshape(2, half, token_rows)
    keep = lax.dynamic_index_in_dim(halves, core, 0, keepdims=False)
    give = lax.dynamic_index_in_dim(halves, 1 - core, 0, keepdims=False)
    features = jnp.concatenate([keep, from_core(give)], axis=1)
    crossed = lax.ppermute(tokens, ("dp", "tensor"), swap_pairs())
    block = jnp.stack([features, crossed])
    line = [block] + [lax.ppermute(block, "tensor", tensor_pairs(0, i)) for i in range(1, RING)]
    line = rolled(jnp.stack(line), (z_hi - z_lo) % RING)
    ring_y = jnp.stack(ring(line, lambda b, s: lax.ppermute(b, "tensor", tensor_pairs(s, 0)), 1))
    ring_y = rolled(ring_y, (x - y) % RING)
    features_all = ring_y[:, :, 0].reshape(-1, 2 * token_rows)
    crossed_all = ring_y[:, :, 1].reshape(-1, 2 * half)

    scaled_pair = jnp.concatenate([scaled, from_core(scaled)], axis=0)
    scaled_all = gather_pairwise(scaled, -1)

    over_rows = (((0,), (0,)), ((), ()))
    over_cols = (((1,), (1,)), ((), ()))

    term = lax.dot_general(weight_all, scaled_pair, over_cols, preferred_element_type=jnp.float32)
    term = rolled(term.astype(jnp.bfloat16).reshape(RING, -1, 2 * token_rows), (y - x) % RING)
    total = term[0].astype(jnp.float32)
    for i in range(1, RING):
        total += lax.ppermute(term[i], "tensor", tensor_pairs(-i, 0)).astype(jnp.float32)
    total = rolled(total.astype(jnp.bfloat16).reshape(RING, -1, 2 * token_rows), (z_lo - z_hi) % RING)
    final = total[0].astype(jnp.float32)
    for i in range(1, RING):
        final += lax.ppermute(total[i], "tensor", tensor_pairs(0, -i)).astype(jnp.float32)
    final = final.astype(jnp.bfloat16)
    mine = final[:, :token_rows]
    other = from_core(final[:, token_rows:])
    input_grad = jnp.concatenate(
        [jnp.where(core == 0, mine, other), jnp.where(core == 0, other, mine)], axis=0
    ).T

    share = lax.dot_general(features_all, weight_all, over_rows, preferred_element_type=jnp.float32)
    running = share[:token_rows] + from_core(share[token_rows:].astype(jnp.bfloat16)).astype(jnp.float32)
    output = (running * col_scale[None, :]).astype(jnp.bfloat16)

    grad_factor = 1.0 / jnp.sqrt(jnp.float32(token_rows * dp_count))
    grads = lax.dot_general(crossed_all, scaled_all, over_rows, preferred_element_type=jnp.float32)
    grads = grads.reshape(2, half, local_cols)
    grad_own = lax.dynamic_index_in_dim(grads, core, 0, keepdims=False)
    grad_other = lax.dynamic_index_in_dim(grads, 1 - core, 0, keepdims=False)
    weight_grad = (grad_own + from_core(grad_other.astype(jnp.bfloat16)).astype(jnp.float32)) * grad_factor
    return (output, input_grad, weight_grad)


def solution(mesh):
    placed = (P("dp", "tensor"), P("dp", "tensor"), P("dp", "tensor"), P())
    return jax.shard_map(
        on_device,
        mesh=mesh,
        in_specs=placed,
        out_specs=(P("dp", "tensor"), P("dp", "tensor"), P("dp", "tensor")),
        check_vma=False,
    )
```

```python
import jax
import jax.numpy as jnp
from jax import lax
from jax.experimental.layout import Layout, with_layout_constraint
from jax.sharding import PartitionSpec as P

BLOCK = 512
RING = 4
PARTS = 32
GROUPS = 16


def dp_of(x, z, core):
    return ((x % RING) * RING + z % RING) * 2 + core


def dp_pairs(dx, dz, flip):
    return [
        (dp_of(x + dx, z + dz, core ^ flip), dp_of(x, z, core))
        for x in range(RING)
        for z in range(RING)
        for core in range(2)
    ]


def swap_pairs():
    return [
        ((chip * 2 + core) * GROUPS + group, (group * 2 + core) * GROUPS + chip)
        for chip in range(GROUPS)
        for core in range(2)
        for group in range(GROUPS)
    ]


def dp_groups_z():
    return [[dp_of(x, z, core) for z in range(RING)] for x in range(RING) for core in range(2)]


def dp_groups_x():
    return [[dp_of(x, z, core) for x in range(RING)] for z in range(RING) for core in range(2)]


def dp_groups_chips():
    return [[dp_of(x, z, core) for x in range(RING) for z in range(RING)] for core in range(2)]


def tensor_groups_y():
    return [[y * RING + z for y in range(RING)] for z in range(RING)]


def tensor_groups_z():
    return [[y * RING + z for z in range(RING)] for y in range(RING)]


def from_core(block):
    return lax.ppermute(block, "dp", dp_pairs(0, 0, 1))


def row_major(array):
    return with_layout_constraint(array, Layout(major_to_minor=tuple(range(array.ndim))))


def exchange(parts, axis, groups):
    parts = row_major(parts)
    return row_major(lax.all_to_all(parts, axis, 0, 0, axis_index_groups=groups, tiled=True))


def collect(block, axis, groups):
    return exchange(jnp.broadcast_to(block[None], (RING,) + block.shape), axis, groups)


def on_device(tokens, weight, cotangent, levels):
    token_rows = tokens.shape[0]
    local_cols = weight.shape[1]
    dp_count = lax.axis_size("dp")
    dp = lax.axis_index("dp")
    tensor = lax.axis_index("tensor")
    core = dp % 2
    half = tokens.shape[1] // 2

    col_start = tensor * local_cols
    column_ids = col_start + jnp.arange(local_cols, dtype=jnp.int32)
    block_ids = column_ids // BLOCK
    block_range = jnp.arange(levels.shape[0], dtype=jnp.int32)
    membership = (block_ids[None, :] == block_range[:, None]).astype(jnp.float32)
    level_vals = levels.astype(jnp.float32) / 8.0
    col_scale = jnp.sum(membership * level_vals[:, None], axis=0)
    scaled = (cotangent.astype(jnp.float32) * col_scale[None, :]).astype(jnp.bfloat16)

    weight_all = lax.all_gather(weight, "dp", axis=0, axis_index_groups=dp_groups_chips(), tiled=True)

    halves = tokens.T.reshape(2, half, token_rows)
    keep = lax.dynamic_index_in_dim(halves, core, 0, keepdims=False)
    give = lax.dynamic_index_in_dim(halves, 1 - core, 0, keepdims=False)
    features = jnp.concatenate([keep, from_core(give)], axis=1)
    crossed = lax.ppermute(tokens, ("dp", "tensor"), swap_pairs())
    block = row_major(jnp.stack([features, crossed]))
    line = collect(block, "tensor", tensor_groups_z())
    square = collect(line, "tensor", tensor_groups_y())
    features_all = square[:, :, 0].reshape(-1, 2 * token_rows)
    crossed_all = square[:, :, 1].reshape(-1, 2 * half)

    scaled_pair = jnp.concatenate([scaled, from_core(scaled)], axis=0)
    scaled_z = collect(scaled, "dp", dp_groups_z())
    scaled_all = collect(scaled_z, "dp", dp_groups_x()).reshape(-1, local_cols)
    weight_all, scaled_all = lax.optimization_barrier((weight_all, scaled_all))

    over_rows = (((0,), (0,)), ((), ()))
    over_cols = (((1,), (1,)), ((), ()))

    term = lax.dot_general(weight_all, scaled_pair, over_cols, preferred_element_type=jnp.float32)
    term = row_major(term.astype(jnp.bfloat16)).reshape(RING, -1, 2 * token_rows)
    total = jnp.sum(exchange(term, "tensor", tensor_groups_y()).astype(jnp.float32), axis=0)
    total = total.astype(jnp.bfloat16).reshape(RING, -1, 2 * token_rows)
    final = jnp.sum(exchange(total, "tensor", tensor_groups_z()).astype(jnp.float32), axis=0)
    final = final.astype(jnp.bfloat16)
    mine = final[:, :token_rows]
    other = from_core(final[:, token_rows:])
    input_grad = jnp.concatenate(
        [jnp.where(core == 0, mine, other), jnp.where(core == 0, other, mine)], axis=0
    ).T

    share = lax.dot_general(features_all, weight_all, over_rows, preferred_element_type=jnp.float32)
    running = share[:token_rows] + from_core(share[token_rows:].astype(jnp.bfloat16)).astype(jnp.float32)
    output = (running * col_scale[None, :]).astype(jnp.bfloat16)

    grad_factor = 1.0 / jnp.sqrt(jnp.float32(token_rows * dp_count))
    grads = lax.dot_general(crossed_all, scaled_all, over_rows, preferred_element_type=jnp.float32)
    grads = grads.reshape(2, half, local_cols)
    grad_own = lax.dynamic_index_in_dim(grads, core, 0, keepdims=False)
    grad_other = lax.dynamic_index_in_dim(grads, 1 - core, 0, keepdims=False)
    weight_grad = (grad_own + from_core(grad_other.astype(jnp.bfloat16)).astype(jnp.float32)) * grad_factor
    return (output, input_grad, weight_grad)


def solution(mesh):
    placed = (P("dp", "tensor"), P("dp", "tensor"), P("dp", "tensor"), P())
    return jax.shard_map(
        on_device,
        mesh=mesh,
        in_specs=placed,
        out_specs=(P("dp", "tensor"), P("dp", "tensor"), P("dp", "tensor")),
        check_vma=False,
    )
```

```python
import jax
import jax.numpy as jnp
from jax import lax
from jax.experimental.layout import Layout, with_layout_constraint
from jax.sharding import PartitionSpec as P

BLOCK = 512
RING = 4
PARTS = 32
GROUPS = 16


def dp_of(x, z, core):
    return ((x % RING) * RING + z % RING) * 2 + core


def dp_pairs(dx, dz, flip):
    return [
        (dp_of(x + dx, z + dz, core ^ flip), dp_of(x, z, core))
        for x in range(RING)
        for z in range(RING)
        for core in range(2)
    ]


def swap_pairs():
    return [
        ((chip * 2 + core) * GROUPS + group, (group * 2 + core) * GROUPS + chip)
        for chip in range(GROUPS)
        for core in range(2)
        for group in range(GROUPS)
    ]


def dp_groups_z():
    return [[dp_of(x, z, core) for z in range(RING)] for x in range(RING) for core in range(2)]


def dp_groups_x():
    return [[dp_of(x, z, core) for x in range(RING)] for z in range(RING) for core in range(2)]


def tensor_groups_y():
    return [[y * RING + z for y in range(RING)] for z in range(RING)]


def tensor_groups_z():
    return [[y * RING + z for z in range(RING)] for y in range(RING)]


def from_core(block):
    return lax.ppermute(block, "dp", dp_pairs(0, 0, 1))


def row_major(array):
    return with_layout_constraint(array, Layout(major_to_minor=tuple(range(array.ndim))))


def exchange(parts, axis, groups):
    parts = row_major(parts)
    return row_major(lax.all_to_all(parts, axis, 0, 0, axis_index_groups=groups, tiled=True))


def collect(block, axis, groups):
    return exchange(jnp.broadcast_to(block[None], (RING,) + block.shape), axis, groups)


def gather_z(block):
    return lax.all_gather(block, "dp", axis=0, axis_index_groups=dp_groups_z(), tiled=True)


def gather_x(block):
    return lax.all_gather(block, "dp", axis=0, axis_index_groups=dp_groups_x(), tiled=True)


def on_device(tokens, weight, cotangent, levels):
    token_rows = tokens.shape[0]
    local_cols = weight.shape[1]
    dp_count = lax.axis_size("dp")
    dp = lax.axis_index("dp")
    tensor = lax.axis_index("tensor")
    core = dp % 2
    half = tokens.shape[1] // 2

    col_start = tensor * local_cols
    column_ids = col_start + jnp.arange(local_cols, dtype=jnp.int32)
    block_ids = column_ids // BLOCK
    block_range = jnp.arange(levels.shape[0], dtype=jnp.int32)
    membership = (block_ids[None, :] == block_range[:, None]).astype(jnp.float32)
    level_vals = levels.astype(jnp.float32) / 8.0
    col_scale = jnp.sum(membership * level_vals[:, None], axis=0)
    scaled = (cotangent.astype(jnp.float32) * col_scale[None, :]).astype(jnp.bfloat16)

    weight, scaled = lax.optimization_barrier((weight, scaled))
    weight_all = gather_x(gather_z(weight))

    halves = tokens.T.reshape(2, half, token_rows)
    keep = lax.dynamic_index_in_dim(halves, core, 0, keepdims=False)
    give = lax.dynamic_index_in_dim(halves, 1 - core, 0, keepdims=False)
    features = jnp.concatenate([keep, from_core(give)], axis=1)
    crossed = lax.ppermute(tokens, ("dp", "tensor"), swap_pairs())
    block = row_major(jnp.stack([features, crossed]))
    line = collect(block, "tensor", tensor_groups_z())
    square = collect(line, "tensor", tensor_groups_y())
    features_all = square[:, :, 0].reshape(-1, 2 * token_rows)
    crossed_all = square[:, :, 1].reshape(-1, 2 * half)

    scaled_pair = jnp.concatenate([scaled, from_core(scaled)], axis=0)
    scaled_line = gather_z(scaled)
    weight_all, scaled_line = lax.optimization_barrier((weight_all, scaled_line))
    scaled_all = gather_x(scaled_line)

    over_rows = (((0,), (0,)), ((), ()))
    over_cols = (((1,), (1,)), ((), ()))

    term = lax.dot_general(weight_all, scaled_pair, over_cols, preferred_element_type=jnp.float32)
    term = row_major(term.astype(jnp.bfloat16)).reshape(RING, -1, 2 * token_rows)
    total = jnp.sum(exchange(term, "tensor", tensor_groups_y()).astype(jnp.float32), axis=0)
    total = total.astype(jnp.bfloat16).reshape(RING, -1, 2 * token_rows)
    final = jnp.sum(exchange(total, "tensor", tensor_groups_z()).astype(jnp.float32), axis=0)
    final = final.astype(jnp.bfloat16)
    mine = final[:, :token_rows]
    other = from_core(final[:, token_rows:])
    input_grad = jnp.concatenate(
        [jnp.where(core == 0, mine, other), jnp.where(core == 0, other, mine)], axis=0
    ).T

    share = lax.dot_general(features_all, weight_all, over_rows, preferred_element_type=jnp.float32)
    running = share[:token_rows] + from_core(share[token_rows:].astype(jnp.bfloat16)).astype(jnp.float32)
    output = (running * col_scale[None, :]).astype(jnp.bfloat16)

    grad_factor = 1.0 / jnp.sqrt(jnp.float32(token_rows * dp_count))
    grads = lax.dot_general(crossed_all, scaled_all, over_rows, preferred_element_type=jnp.float32)
    grads = grads.reshape(2, half, local_cols)
    grad_own = lax.dynamic_index_in_dim(grads, core, 0, keepdims=False)
    grad_other = lax.dynamic_index_in_dim(grads, 1 - core, 0, keepdims=False)
    weight_grad = (grad_own + from_core(grad_other.astype(jnp.bfloat16)).astype(jnp.float32)) * grad_factor
    return (output, input_grad, weight_grad)


def solution(mesh):
    placed = (P("dp", "tensor"), P("dp", "tensor"), P("dp", "tensor"), P())
    return jax.shard_map(
        on_device,
        mesh=mesh,
        in_specs=placed,
        out_specs=(P("dp", "tensor"), P("dp", "tensor"), P("dp", "tensor")),
        check_vma=False,
    )
```

```python
import jax
import jax.numpy as jnp
from jax import lax
from jax.experimental.layout import Layout, with_layout_constraint
from jax.sharding import PartitionSpec as P

BLOCK = 512
RING = 4
GROUPS = 16


def dp_of(x, z, core):
    return ((x % RING) * RING + z % RING) * 2 + core


def dp_pairs(dz, flip):
    return [
        (dp_of(x, z + dz, core ^ flip), dp_of(x, z, core))
        for x in range(RING)
        for z in range(RING)
        for core in range(2)
    ]


def swap_pairs(flip):
    return [
        (
            dp_of(y, z, core ^ flip) * GROUPS + x * RING + low,
            dp_of(x, z, core) * GROUPS + y * RING + low,
        )
        for x in range(RING)
        for z in range(RING)
        for core in range(2)
        for y in range(RING)
        for low in range(RING)
    ]


def groups_x():
    return [[dp_of(x, z, core) for x in range(RING)] for z in range(RING) for core in range(2)]


def groups_y():
    return [[y * RING + low for y in range(RING)] for low in range(RING)]


def groups_low():
    return [[y * RING + low for low in range(RING)] for y in range(RING)]


def from_core(block):
    return lax.ppermute(block, "dp", dp_pairs(0, 1))


def from_z(block, shift):
    return lax.ppermute(block, "dp", dp_pairs(shift, 0))


def from_swap(block, flip):
    return lax.ppermute(block, ("dp", "tensor"), swap_pairs(flip))


def row_major(array):
    return with_layout_constraint(array, Layout(major_to_minor=tuple(range(array.ndim))))


def exchange(parts, axis, groups):
    parts = row_major(parts)
    return row_major(lax.all_to_all(parts, axis, 0, 0, axis_index_groups=groups, tiled=True))


def collect(block, axis, groups):
    return exchange(jnp.broadcast_to(block[None], (RING,) + block.shape), axis, groups)


def rolled(array, start):
    return lax.dynamic_slice_in_dim(jnp.concatenate([array, array], axis=0), start, array.shape[0], 0)


def total(parts):
    return jnp.sum(parts.astype(jnp.float32), axis=0)


def on_device(tokens, weight, cotangent, levels):
    token_rows, local_features = tokens.shape
    local_cols = weight.shape[1]
    half = local_features // 2
    dp_count = lax.axis_size("dp")
    dp = lax.axis_index("dp")
    tensor = lax.axis_index("tensor")
    core = dp % 2
    z_hi = (dp // 2) % RING
    wide = jnp.float32
    narrow = jnp.bfloat16

    col_start = tensor * local_cols
    column_ids = col_start + jnp.arange(local_cols, dtype=jnp.int32)
    block_ids = column_ids // BLOCK
    block_range = jnp.arange(levels.shape[0], dtype=jnp.int32)
    membership = (block_ids[None, :] == block_range[:, None]).astype(wide)
    level_vals = levels.astype(wide) / 8.0
    col_scale = jnp.sum(membership * level_vals[:, None], axis=0)

    scaled = (cotangent.astype(wide) * col_scale[None, :]).astype(narrow)
    tokens, scaled = lax.optimization_barrier((tokens, scaled))

    ahead = from_z(weight, 1)
    behind = from_z(weight, -1)
    mid = weight.shape[0] // 2
    far_top = from_z(ahead[:mid], 1)
    far_low = from_z(behind[mid:], -1)
    weight_line = jnp.concatenate([weight, ahead, far_top, far_low, behind], axis=0)

    keep = lax.dynamic_slice_in_dim(tokens, core * half, half, 1)
    give = lax.dynamic_slice_in_dim(tokens, (1 - core) * half, half, 1)
    pair = row_major(jnp.stack([from_swap(keep, 0), from_swap(give, 1)]))
    line = rolled(collect(pair, "tensor", groups_low()), z_hi).reshape(RING, 2 * token_rows, half)
    line = jnp.concatenate([line[i] for i in range(RING)], axis=1)
    brick = collect(line, "tensor", groups_y()).reshape(-1, RING * half)

    scaled_own = collect(scaled, "dp", groups_x())
    scaled_all = jnp.stack([scaled_own, from_core(scaled_own)], axis=1).reshape(-1, local_cols)

    grads = lax.dot_general(brick, scaled_all, (((0,), (0,)), ((), ())), preferred_element_type=wide)
    grads = grads.reshape(RING, 2, mid, local_cols)
    far = grads[2].astype(narrow)
    far, weight_line = lax.optimization_barrier((far, weight_line))
    top = from_z(far[0], -1).astype(wide)
    low = from_z(far[1], 1).astype(wide)
    up = jnp.stack([grads[1, 0] + top, grads[1, 1]]).astype(narrow)
    down = jnp.stack([grads[3, 0], grads[3, 1] + low]).astype(narrow)
    grad_sum = grads[0] + from_z(up, -1).astype(wide) + from_z(down, 1).astype(wide)
    grad_factor = 1.0 / jnp.sqrt(jnp.float32(token_rows * dp_count))
    weight_grad = grad_sum.reshape(-1, local_cols) * grad_factor

    term = lax.dot_general(scaled_all, weight_line, (((1,), (1,)), ((), ())), preferred_element_type=wide)
    term = row_major(term.astype(narrow)).reshape(RING, 2 * token_rows, RING * half)
    term = total(exchange(term, "tensor", groups_y()))
    term = term.astype(narrow)
    term = jnp.stack([term[:, i * half:(i + 1) * half] for i in range(RING)])
    term = rolled(term, (RING - z_hi) % RING)
    term = total(exchange(term, "tensor", groups_low())).astype(narrow)
    mine = from_swap(term[:token_rows], 0)
    other = from_swap(term[token_rows:], 1)
    input_grad = jnp.concatenate(
        [jnp.where(core == 0, mine, other), jnp.where(core == 0, other, mine)], axis=1
    )

    share = jnp.dot(brick, weight_line, preferred_element_type=wide)
    share = share.reshape(RING, 2, token_rows, local_cols)
    share = share[:, 0] + from_core(share[:, 1].astype(narrow)).astype(wide)
    running = total(exchange(share.astype(narrow), "dp", groups_x()))
    output = (running * col_scale[None, :]).astype(narrow)
    return (output, input_grad, weight_grad)


def solution(mesh):
    placed = (P("dp", "tensor"), P("dp", "tensor"), P("dp", "tensor"), P())
    return jax.shard_map(
        on_device,
        mesh=mesh,
        in_specs=placed,
        out_specs=(P("dp", "tensor"), P("dp", "tensor"), P("dp", "tensor")),
        check_vma=False,
    )
```

```python
import jax
import jax.numpy as jnp
from jax import lax
from jax.experimental.layout import Layout, with_layout_constraint
from jax.sharding import PartitionSpec as P

BLOCK = 512
RING = 4
GROUPS = 16


def dp_of(x, z, core):
    return ((x % RING) * RING + z % RING) * 2 + core


def swap_pairs():
    return [
        (
            dp_of(y, z, core) * GROUPS + x * RING + low,
            dp_of(x, z, core) * GROUPS + y * RING + low,
        )
        for x in range(RING)
        for z in range(RING)
        for core in range(2)
        for y in range(RING)
        for low in range(RING)
    ]


def groups_z():
    return [[dp_of(x, z, core) for z in range(RING)] for x in range(RING) for core in range(2)]


def groups_x_core():
    return [[dp_of(x, z, core) for x in range(RING) for core in range(2)] for z in range(RING)]


def groups_y():
    return [[y * RING + low for y in range(RING)] for low in range(RING)]


def groups_core_low():
    return [
        [dp_of(x, z, core) * GROUPS + y * RING + low for core in range(2) for low in range(RING)]
        for x in range(RING)
        for z in range(RING)
        for y in range(RING)
    ]


def swap(block):
    return lax.ppermute(block, ("dp", "tensor"), swap_pairs())


def row_major(array):
    return with_layout_constraint(array, Layout(major_to_minor=tuple(range(array.ndim))))


def exchange(parts, axis, groups):
    parts = row_major(parts)
    return row_major(lax.all_to_all(parts, axis, 0, 0, axis_index_groups=groups, tiled=True))


def collect(block, axis, groups):
    return exchange(jnp.broadcast_to(block[None], (len(groups[0]),) + block.shape), axis, groups)


def total(parts):
    return jnp.sum(parts.astype(jnp.float32), axis=0)


def on_device(tokens, weight, cotangent, levels):
    token_rows, local_features = tokens.shape
    local_cols = weight.shape[1]
    half = local_features // 2
    dp_count = lax.axis_size("dp")
    tensor = lax.axis_index("tensor")
    wide = jnp.float32
    narrow = jnp.bfloat16

    col_start = tensor * local_cols
    column_ids = col_start + jnp.arange(local_cols, dtype=jnp.int32)
    block_ids = column_ids // BLOCK
    block_range = jnp.arange(levels.shape[0], dtype=jnp.int32)
    membership = (block_ids[None, :] == block_range[:, None]).astype(wide)
    level_vals = levels.astype(wide) / 8.0
    col_scale = jnp.sum(membership * level_vals[:, None], axis=0)

    scaled = (cotangent.astype(wide) * col_scale[None, :]).astype(narrow)
    weight_line = collect(weight, "dp", groups_z()).reshape(-1, local_cols)

    scaled_all = collect(scaled, "dp", groups_x_core()).reshape(-1, local_cols)

    both = ("dp", "tensor")
    crossed = swap(tokens)
    parts = jnp.stack([crossed[:, :half]] * RING + [crossed[:, half:]] * RING)
    line = exchange(parts, both, groups_core_low())
    line = line.reshape(2, RING, token_rows, half)
    line = jnp.concatenate([line[:, i] for i in range(RING)], axis=2)
    brick = collect(line, "tensor", groups_y()).reshape(-1, RING * half)

    grads = lax.dot_general(brick, scaled_all, (((0,), (0,)), ((), ())), preferred_element_type=wide)
    grads = grads.astype(narrow).reshape(RING, half, local_cols)
    grads, weight_line = lax.optimization_barrier((grads, weight_line))
    grad_factor = 1.0 / jnp.sqrt(jnp.float32(token_rows * dp_count))
    weight_grad = total(exchange(grads, "dp", groups_z())) * grad_factor

    term = lax.dot_general(scaled_all, weight_line, (((1,), (1,)), ((), ())), preferred_element_type=wide)
    term = row_major(term.astype(narrow)).reshape(RING, 2, token_rows, RING * half)
    term = total(exchange(term, "tensor", groups_y())).astype(narrow)
    term = jnp.stack([term[c, :, i * half:(i + 1) * half] for c in range(2) for i in range(RING)])
    term = exchange(term, both, groups_core_low()).reshape(2, RING, token_rows, half)
    term = jnp.sum(term.astype(wide), axis=1).astype(narrow)
    input_grad = swap(jnp.concatenate([term[0], term[1]], axis=1))

    share = jnp.dot(brick, weight_line, preferred_element_type=wide).astype(narrow)
    running = total(exchange(share.reshape(2 * RING, token_rows, local_cols), "dp", groups_x_core()))
    output = (running * col_scale[None, :]).astype(narrow)
    return (output, input_grad, weight_grad)


def solution(mesh):
    placed = (P("dp", "tensor"), P("dp", "tensor"), P("dp", "tensor"), P())
    return jax.shard_map(
        on_device,
        mesh=mesh,
        in_specs=placed,
        out_specs=(P("dp", "tensor"), P("dp", "tensor"), P("dp", "tensor")),
        check_vma=False,
    )
```

```python
import jax
import jax.numpy as jnp
from jax import lax
from jax.experimental.layout import Layout, with_layout_constraint
from jax.sharding import PartitionSpec as P

BLOCK = 512
RING = 4
GROUPS = 16


def dp_of(x, z, core):
    return ((x % RING) * RING + z % RING) * 2 + core


def swap_pairs():
    return [
        (
            dp_of(y, z, core) * GROUPS + x * RING + low,
            dp_of(x, z, core) * GROUPS + y * RING + low,
        )
        for x in range(RING)
        for z in range(RING)
        for core in range(2)
        for y in range(RING)
        for low in range(RING)
    ]


def dp_pairs(dx, dz, flip):
    return [
        (dp_of(x + dx, z + dz, core ^ flip), dp_of(x, z, core))
        for x in range(RING)
        for z in range(RING)
        for core in range(2)
    ]


def groups_x():
    return [[dp_of(x, z, core) for x in range(RING)] for z in range(RING) for core in range(2)]


def groups_y():
    return [[y * RING + low for y in range(RING)] for low in range(RING)]


def groups_core_low():
    return [
        [
            dp_of(x, z, core) * GROUPS + y * RING + (z + i) % RING
            for core in range(2)
            for i in range(RING)
        ]
        for x in range(RING)
        for z in range(RING)
        for y in range(RING)
    ]


def from_core(block):
    return lax.ppermute(block, "dp", dp_pairs(0, 0, 1))


def from_x(block, shift):
    return lax.ppermute(block, "dp", dp_pairs(shift, 0, 0))


def from_z(block, shift):
    return lax.ppermute(block, "dp", dp_pairs(0, shift, 0))


def swap(block):
    return lax.ppermute(block, ("dp", "tensor"), swap_pairs())


def row_major(array):
    return with_layout_constraint(array, Layout(major_to_minor=tuple(range(array.ndim))))


def exchange(parts, axis, groups):
    parts = row_major(parts)
    return row_major(lax.all_to_all(parts, axis, 0, 0, axis_index_groups=groups, tiled=True))


def collect(block, axis, groups):
    return exchange(jnp.broadcast_to(block[None], (len(groups[0]),) + block.shape), axis, groups)


def total(parts):
    return jnp.sum(parts.astype(jnp.float32), axis=0)


def near_first(pair, core):
    return jnp.where(core == 0, pair, pair[::-1])


def on_device(tokens, weight, cotangent, levels):
    token_rows, local_features = tokens.shape
    local_cols = weight.shape[1]
    half = local_features // 2
    dp_count = lax.axis_size("dp")
    dp = lax.axis_index("dp")
    core = dp % 2
    x = dp // (2 * RING)
    tensor = lax.axis_index("tensor")
    wide = jnp.float32
    narrow = jnp.bfloat16

    col_start = tensor * local_cols
    column_ids = col_start + jnp.arange(local_cols, dtype=jnp.int32)
    block_ids = column_ids // BLOCK
    block_range = jnp.arange(levels.shape[0], dtype=jnp.int32)
    membership = (block_ids[None, :] == block_range[:, None]).astype(wide)
    level_vals = levels.astype(wide) / 8.0
    col_scale = jnp.sum(membership * level_vals[:, None], axis=0)

    scaled = (cotangent.astype(wide) * col_scale[None, :]).astype(narrow)
    weight_line = [weight] + [from_z(weight, i) for i in range(1, RING)]
    weight_line = jnp.concatenate(weight_line, axis=0)

    scaled_own = collect(scaled, "dp", groups_x())
    scaled_all = jnp.stack([scaled_own, from_core(scaled_own)], axis=1).reshape(-1, local_cols)

    both = ("dp", "tensor")
    crossed = swap(tokens)
    parts = jnp.stack([crossed[:, :half], crossed[:, half:]])
    parts = jnp.broadcast_to(parts[:, None], (2, RING, token_rows, half))
    line = exchange(parts.reshape(2 * RING, token_rows, half), both, groups_core_low())
    line = line.reshape(2, RING, token_rows, half)
    line = jnp.concatenate([line[:, i] for i in range(RING)], axis=2)
    line = near_first(line, core)
    brick = collect(line, "tensor", groups_y()).reshape(-1, RING * half)

    grads = lax.dot_general(brick, scaled_all, (((0,), (0,)), ((), ())), preferred_element_type=wide)
    grads = grads.reshape(RING, half, local_cols)
    away = [grads[i].astype(narrow) for i in range(1, RING)]
    away, weight_line = lax.optimization_barrier((away, weight_line))
    grad_sum = grads[0]
    for i in range(1, RING):
        grad_sum += from_z(away[i - 1], -i).astype(wide)
    grad_factor = 1.0 / jnp.sqrt(jnp.float32(token_rows * dp_count))
    weight_grad = grad_sum * grad_factor

    term = lax.dot_general(scaled_all, weight_line, (((1,), (1,)), ((), ())), preferred_element_type=wide)
    term = row_major(term.astype(narrow)).reshape(RING, 2, token_rows, RING * half)
    term = near_first(total(exchange(term, "tensor", groups_y())).astype(narrow), core)
    term = jnp.stack([term[c, :, i * half:(i + 1) * half] for c in range(2) for i in range(RING)])
    term = exchange(term, both, groups_core_low()).reshape(2, RING, token_rows, half)
    term = jnp.sum(term.astype(wide), axis=1).astype(narrow)
    input_grad = swap(jnp.concatenate([term[0], term[1]], axis=1))

    share = jnp.dot(brick, weight_line, preferred_element_type=wide)
    share = share.reshape(RING, 2, token_rows, local_cols)
    other = from_core(share[:, 1].astype(narrow)).astype(wide)
    running = None
    for i in range(RING):
        at = (x + i) % RING
        part = lax.dynamic_index_in_dim(share[:, 0], at, 0, keepdims=False)
        part += lax.dynamic_index_in_dim(other, at, 0, keepdims=False)
        running = part if i == 0 else running + from_x(part.astype(narrow), -i).astype(wide)
    output = (running * col_scale[None, :]).astype(narrow)
    return (output, input_grad, weight_grad)


def solution(mesh):
    placed = (P("dp", "tensor"), P("dp", "tensor"), P("dp", "tensor"), P())
    return jax.shard_map(
        on_device,
        mesh=mesh,
        in_specs=placed,
        out_specs=(P("dp", "tensor"), P("dp", "tensor"), P("dp", "tensor")),
        check_vma=False,
    )
```

```python
import jax
import jax.numpy as jnp
from jax import lax
from jax.experimental.layout import Layout, with_layout_constraint
from jax.sharding import PartitionSpec as P

BLOCK = 512
RING = 4
GROUPS = 16


def dp_of(x, z, core):
    return ((x % RING) * RING + z % RING) * 2 + core


def swap_pairs():
    return [
        (
            dp_of(y, z, core) * GROUPS + x * RING + low,
            dp_of(x, z, core) * GROUPS + y * RING + low,
        )
        for x in range(RING)
        for z in range(RING)
        for core in range(2)
        for y in range(RING)
        for low in range(RING)
    ]


def dp_pairs(dz, flip):
    return [
        (dp_of(x, z + dz, core ^ flip), dp_of(x, z, core))
        for x in range(RING)
        for z in range(RING)
        for core in range(2)
    ]


def groups_x():
    return [[dp_of(x, z, core) for x in range(RING)] for z in range(RING) for core in range(2)]


def groups_y():
    return [[y * RING + low for y in range(RING)] for low in range(RING)]


def groups_core_low():
    return [
        [
            dp_of(x, z, core) * GROUPS + y * RING + (z + i) % RING
            for core in range(2)
            for i in range(RING)
        ]
        for x in range(RING)
        for z in range(RING)
        for y in range(RING)
    ]


def from_core(block):
    return lax.ppermute(block, "dp", dp_pairs(0, 1))


def from_z(block, shift):
    return lax.ppermute(block, "dp", dp_pairs(shift, 0))


def swap(block):
    return lax.ppermute(block, ("dp", "tensor"), swap_pairs())


def row_major(array):
    return with_layout_constraint(array, Layout(major_to_minor=tuple(range(array.ndim))))


def exchange(parts, axis, groups):
    parts = row_major(parts)
    return row_major(lax.all_to_all(parts, axis, 0, 0, axis_index_groups=groups, tiled=True))


def collect(block, axis, groups):
    return exchange(jnp.broadcast_to(block[None], (len(groups[0]),) + block.shape), axis, groups)


def total(parts):
    return jnp.sum(parts.astype(jnp.float32), axis=0)


def block_of(steps, index, *operands):
    shapes = jax.eval_shape(steps, *operands)

    def nothing(*_):
        return jax.tree.map(lambda leaf: jnp.zeros(leaf.shape, leaf.dtype), shapes)

    return lax.cond(index >= 0, steps, nothing, *operands)


def near_first(pair, core):
    return jnp.where(core == 0, pair, pair[::-1])


def on_device(tokens, weight, cotangent, levels):
    token_rows, local_features = tokens.shape
    local_cols = weight.shape[1]
    half = local_features // 2
    dp_count = lax.axis_size("dp")
    dp = lax.axis_index("dp")
    core = dp % 2
    tensor = lax.axis_index("tensor")
    wide = jnp.float32
    narrow = jnp.bfloat16

    col_start = tensor * local_cols
    column_ids = col_start + jnp.arange(local_cols, dtype=jnp.int32)
    block_ids = column_ids // BLOCK
    block_range = jnp.arange(levels.shape[0], dtype=jnp.int32)
    membership = (block_ids[None, :] == block_range[:, None]).astype(wide)
    level_vals = levels.astype(wide) / 8.0
    col_scale = jnp.sum(membership * level_vals[:, None], axis=0)

    scaled = (cotangent.astype(wide) * col_scale[None, :]).astype(narrow)
    weight_line = [weight] + [from_z(weight, i) for i in range(1, RING)]
    weight_line = jnp.concatenate(weight_line, axis=0)

    both = ("dp", "tensor")

    def inputs(tokens, scaled):
        scaled_own = collect(scaled, "dp", groups_x())
        scaled_all = jnp.stack([scaled_own, from_core(scaled_own)], axis=1).reshape(-1, local_cols)

        crossed = swap(tokens)
        parts = jnp.stack([crossed[:, :half], crossed[:, half:]])
        parts = jnp.broadcast_to(parts[:, None], (2, RING, token_rows, half))
        line = exchange(parts.reshape(2 * RING, token_rows, half), both, groups_core_low())
        line = line.reshape(2, RING, token_rows, half)
        line = jnp.concatenate([line[:, i] for i in range(RING)], axis=2)
        line = near_first(line, core)
        brick = collect(line, "tensor", groups_y()).reshape(-1, RING * half)
        return scaled_all, brick

    scaled_all, brick = block_of(inputs, dp, tokens, scaled)

    grads = lax.dot_general(brick, scaled_all, (((0,), (0,)), ((), ())), preferred_element_type=wide)
    grads = grads.reshape(RING, half, local_cols)
    away = [grads[i].astype(narrow) for i in range(1, RING)]
    away, weight_line = lax.optimization_barrier((away, weight_line))
    received = [from_z(away[i - 1], -i) for i in range(1, RING)]

    def sums(scaled_all, brick, weight_line):
        term = lax.dot_general(scaled_all, weight_line, (((1,), (1,)), ((), ())), preferred_element_type=wide)
        term = row_major(term.astype(narrow)).reshape(RING, 2, token_rows, RING * half)
        term = near_first(total(exchange(term, "tensor", groups_y())).astype(narrow), core)
        term = jnp.stack([term[c, :, i * half:(i + 1) * half] for c in range(2) for i in range(RING)])
        term = exchange(term, both, groups_core_low()).reshape(2, RING, token_rows, half)
        term = jnp.sum(term.astype(wide), axis=1).astype(narrow)
        input_grad = swap(jnp.concatenate([term[0], term[1]], axis=1))

        share = jnp.dot(brick, weight_line, preferred_element_type=wide)
        share = share.reshape(RING, 2, token_rows, local_cols)
        share = share[:, 0] + from_core(share[:, 1].astype(narrow)).astype(wide)
        running = total(exchange(share.astype(narrow), "dp", groups_x()))
        return running, input_grad

    running, input_grad = block_of(sums, dp, scaled_all, brick, weight_line)
    received, running, input_grad = lax.optimization_barrier((received, running, input_grad))
    output = (running * col_scale[None, :]).astype(narrow)
    grad_sum = grads[0]
    for part in received:
        grad_sum += part.astype(wide)
    grad_factor = 1.0 / jnp.sqrt(jnp.float32(token_rows * dp_count))
    weight_grad = grad_sum * grad_factor
    return (output, input_grad, weight_grad)


def solution(mesh):
    placed = (P("dp", "tensor"), P("dp", "tensor"), P("dp", "tensor"), P())
    return jax.shard_map(
        on_device,
        mesh=mesh,
        in_specs=placed,
        out_specs=(P("dp", "tensor"), P("dp", "tensor"), P("dp", "tensor")),
        check_vma=False,
    )
```

```python
import jax
import jax.numpy as jnp
from jax import lax
from jax.experimental.layout import Layout, with_layout_constraint
from jax.sharding import PartitionSpec as P

BLOCK = 512
RING = 4
GROUPS = 16


def dp_of(x, z, core):
    return ((x % RING) * RING + z % RING) * 2 + core


def swap_pairs():
    return [
        (
            dp_of(y, z, core) * GROUPS + x * RING + low,
            dp_of(x, z, core) * GROUPS + y * RING + low,
        )
        for x in range(RING)
        for z in range(RING)
        for core in range(2)
        for y in range(RING)
        for low in range(RING)
    ]


def dp_pairs(dz, flip):
    return [
        (dp_of(x, z + dz, core ^ flip), dp_of(x, z, core))
        for x in range(RING)
        for z in range(RING)
        for core in range(2)
    ]


def groups_x():
    return [[dp_of(x, z, core) for x in range(RING)] for z in range(RING) for core in range(2)]


def groups_y():
    return [[y * RING + low for y in range(RING)] for low in range(RING)]


def groups_core_low():
    return [
        [
            dp_of(x, z, core) * GROUPS + y * RING + (z + i) % RING
            for i in range(RING)
            for core in range(2)
        ]
        for x in range(RING)
        for z in range(RING)
        for y in range(RING)
    ]


def from_core(block):
    return lax.ppermute(block, "dp", dp_pairs(0, 1))


def from_z(block, shift):
    return lax.ppermute(block, "dp", dp_pairs(shift, 0))


def swap(block):
    return lax.ppermute(block, ("dp", "tensor"), swap_pairs())


def row_major(array):
    return with_layout_constraint(array, Layout(major_to_minor=tuple(range(array.ndim))))


def exchange(parts, axis, groups):
    parts = row_major(parts)
    return row_major(lax.all_to_all(parts, axis, 0, 0, axis_index_groups=groups, tiled=True))


def collect(block, axis, groups):
    return exchange(jnp.broadcast_to(block[None], (len(groups[0]),) + block.shape), axis, groups)


def total(parts):
    return jnp.sum(parts.astype(jnp.float32), axis=0)


def block_of(steps, index, *operands):
    shapes = jax.eval_shape(steps, *operands)

    def nothing(*_):
        return jax.tree.map(lambda leaf: jnp.zeros(leaf.shape, leaf.dtype), shapes)

    return lax.cond(index >= 0, steps, nothing, *operands)


def near_first(pair, core):
    return jnp.where(core == 0, pair, pair[::-1])


def on_device(tokens, weight, cotangent, levels):
    token_rows, local_features = tokens.shape
    local_cols = weight.shape[1]
    half = local_features // 2
    dp_count = lax.axis_size("dp")
    dp = lax.axis_index("dp")
    core = dp % 2
    tensor = lax.axis_index("tensor")
    wide = jnp.float32
    narrow = jnp.bfloat16

    col_start = tensor * local_cols
    column_ids = col_start + jnp.arange(local_cols, dtype=jnp.int32)
    block_ids = column_ids // BLOCK
    block_range = jnp.arange(levels.shape[0], dtype=jnp.int32)
    membership = (block_ids[None, :] == block_range[:, None]).astype(wide)
    level_vals = levels.astype(wide) / 8.0
    col_scale = jnp.sum(membership * level_vals[:, None], axis=0)

    scaled = (cotangent.astype(wide) * col_scale[None, :]).astype(narrow)
    weight_line = [weight] + [from_z(weight, i) for i in range(1, RING)]
    weight_line = jnp.concatenate(weight_line, axis=0)

    scaled_own = collect(scaled, "dp", groups_x())
    crossed = swap(tokens)
    both = ("dp", "tensor")

    def inputs(crossed, scaled_own):
        scaled_all = jnp.stack([scaled_own, from_core(scaled_own)], axis=1).reshape(-1, local_cols)

        parts = jnp.stack([crossed[:, :half], crossed[:, half:]])
        parts = jnp.broadcast_to(parts[None], (RING, 2, token_rows, half))
        line = exchange(parts.reshape(2 * RING, token_rows, half), both, groups_core_low())
        line = line.reshape(RING, 2, token_rows, half)
        line = jnp.concatenate([line[i] for i in range(RING)], axis=2)
        line = near_first(line, core)
        brick = collect(line, "tensor", groups_y()).reshape(-1, RING * half)
        return scaled_all, brick

    scaled_all, brick = block_of(inputs, dp, crossed, scaled_own)

    grads = lax.dot_general(brick, scaled_all, (((0,), (0,)), ((), ())), preferred_element_type=wide)
    grads = grads.reshape(RING, half, local_cols)
    away = [grads[i].astype(narrow) for i in range(1, RING)]
    away, weight_line = lax.optimization_barrier((away, weight_line))
    received = [from_z(away[i - 1], -i) for i in range(1, RING)]

    term = lax.dot_general(scaled_all, weight_line, (((1,), (1,)), ((), ())), preferred_element_type=wide)
    term = row_major(term.astype(narrow)).reshape(RING, 2, token_rows, RING * half)
    term = exchange(term, "tensor", groups_y())

    share = jnp.dot(brick, weight_line, preferred_element_type=wide)

    def sums(term, share):
        term = near_first(total(term).astype(narrow), core)
        term = jnp.stack([term[:, :, i * half:(i + 1) * half] for i in range(RING)])
        term = exchange(term.reshape(2 * RING, token_rows, half), both, groups_core_low())
        term = total(term.reshape(RING, 2, token_rows, half)).astype(narrow)
        input_grad = swap(jnp.concatenate([term[0], term[1]], axis=1))

        share = share.reshape(RING, 2, token_rows, local_cols)
        share = share[:, 0] + from_core(share[:, 1].astype(narrow)).astype(wide)
        running = total(exchange(share.astype(narrow), "dp", groups_x()))
        return running, input_grad

    running, input_grad = block_of(sums, dp, term, share)
    received, running, input_grad = lax.optimization_barrier((received, running, input_grad))
    output = (running * col_scale[None, :]).astype(narrow)
    grad_sum = grads[0]
    for part in received:
        grad_sum += part.astype(wide)
    grad_factor = 1.0 / jnp.sqrt(jnp.float32(token_rows * dp_count))
    weight_grad = grad_sum * grad_factor
    return (output, input_grad, weight_grad)


def solution(mesh):
    placed = (P("dp", "tensor"), P("dp", "tensor"), P("dp", "tensor"), P())
    return jax.shard_map(
        on_device,
        mesh=mesh,
        in_specs=placed,
        out_specs=(P("dp", "tensor"), P("dp", "tensor"), P("dp", "tensor")),
        check_vma=False,
    )
```

```python
import jax
import jax.numpy as jnp
from jax import lax
from jax.experimental.layout import Layout, with_layout_constraint
from jax.sharding import PartitionSpec as P

BLOCK = 512
RING = 4
GROUPS = 16


def dp_of(x, z, core):
    return ((x % RING) * RING + z % RING) * 2 + core


def swap_pairs():
    return [
        (
            dp_of(y, z, core) * GROUPS + x * RING + low,
            dp_of(x, z, core) * GROUPS + y * RING + low,
        )
        for x in range(RING)
        for z in range(RING)
        for core in range(2)
        for y in range(RING)
        for low in range(RING)
    ]


def dp_pairs(dz, flip):
    return [
        (dp_of(x, z + dz, core ^ flip), dp_of(x, z, core))
        for x in range(RING)
        for z in range(RING)
        for core in range(2)
    ]


def groups_x():
    return [[dp_of(x, z, core) for x in range(RING)] for z in range(RING) for core in range(2)]


def groups_y():
    return [[y * RING + low for y in range(RING)] for low in range(RING)]


def groups_core_low():
    return [
        [
            dp_of(x, z, core) * GROUPS + y * RING + (z + i) % RING
            for i in range(RING)
            for core in range(2)
        ]
        for x in range(RING)
        for z in range(RING)
        for y in range(RING)
    ]


def from_core(block):
    return lax.ppermute(block, "dp", dp_pairs(0, 1))


def from_z(block, shift):
    return lax.ppermute(block, "dp", dp_pairs(shift, 0))


def swap(block):
    return lax.ppermute(block, ("dp", "tensor"), swap_pairs())


def row_major(array):
    return with_layout_constraint(array, Layout(major_to_minor=tuple(range(array.ndim))))


def exchange(parts, axis, groups):
    parts = row_major(parts)
    return row_major(lax.all_to_all(parts, axis, 0, 0, axis_index_groups=groups, tiled=True))


def collect(block, axis, groups):
    return exchange(jnp.broadcast_to(block[None], (len(groups[0]),) + block.shape), axis, groups)


def total(parts):
    return jnp.sum(parts.astype(jnp.float32), axis=0)


def block_of(steps, index, *operands):
    shapes = jax.eval_shape(steps, *operands)

    def nothing(*_):
        return jax.tree.map(lambda leaf: jnp.zeros(leaf.shape, leaf.dtype), shapes)

    return lax.cond(index >= 0, steps, nothing, *operands)


def near_first(pair, core):
    return jnp.where(core == 0, pair, pair[::-1])


def on_device(tokens, weight, cotangent, levels):
    token_rows, local_features = tokens.shape
    local_cols = weight.shape[1]
    half = local_features // 2
    dp_count = lax.axis_size("dp")
    dp = lax.axis_index("dp")
    core = dp % 2
    tensor = lax.axis_index("tensor")
    wide = jnp.float32
    narrow = jnp.bfloat16

    col_start = tensor * local_cols
    column_ids = col_start + jnp.arange(local_cols, dtype=jnp.int32)
    block_ids = column_ids // BLOCK
    block_range = jnp.arange(levels.shape[0], dtype=jnp.int32)
    membership = (block_ids[None, :] == block_range[:, None]).astype(wide)
    level_vals = levels.astype(wide) / 8.0
    col_scale = jnp.sum(membership * level_vals[:, None], axis=0)

    scaled = (cotangent.astype(wide) * col_scale[None, :]).astype(narrow)
    weight_line = [weight] + [from_z(weight, i) for i in range(1, RING)]
    weight_line = jnp.concatenate(weight_line, axis=0)

    scaled_pair = jnp.concatenate([scaled, from_core(scaled)], axis=0)
    scaled_all = lax.all_gather(scaled_pair, "dp", axis=0, axis_index_groups=groups_x(), tiled=True)

    both = ("dp", "tensor")

    def inputs(tokens):
        crossed = swap(tokens)
        parts = jnp.stack([crossed[:, :half], crossed[:, half:]])
        parts = jnp.broadcast_to(parts[None], (RING, 2, token_rows, half))
        line = exchange(parts.reshape(2 * RING, token_rows, half), both, groups_core_low())
        line = line.reshape(RING, 2, token_rows, half)
        line = jnp.concatenate([line[i] for i in range(RING)], axis=2)
        line = near_first(line, core)
        return collect(line, "tensor", groups_y()).reshape(-1, RING * half)

    brick = block_of(inputs, dp, tokens)

    grads = lax.dot_general(brick, scaled_all, (((0,), (0,)), ((), ())), preferred_element_type=wide)
    grads = grads.reshape(RING, half, local_cols)
    away = [grads[i].astype(narrow) for i in range(1, RING)]
    away, weight_line = lax.optimization_barrier((away, weight_line))
    received = [from_z(away[i - 1], -i) for i in range(1, RING)]

    share = jnp.dot(brick, weight_line, preferred_element_type=wide).astype(narrow)
    share, scaled_all = lax.optimization_barrier((share, scaled_all))
    share = lax.psum_scatter(
        share, "dp", scatter_dimension=0, axis_index_groups=groups_x(), tiled=True
    )

    def sums(scaled_all, weight_line):
        term = lax.dot_general(scaled_all, weight_line, (((1,), (1,)), ((), ())), preferred_element_type=wide)
        term = row_major(term.astype(narrow)).reshape(RING, 2, token_rows, RING * half)
        term = near_first(total(exchange(term, "tensor", groups_y())).astype(narrow), core)
        term = jnp.stack([term[:, :, i * half:(i + 1) * half] for i in range(RING)])
        term = exchange(term.reshape(2 * RING, token_rows, half), both, groups_core_low())
        term = total(term.reshape(RING, 2, token_rows, half)).astype(narrow)
        return swap(jnp.concatenate([term[0], term[1]], axis=1))

    input_grad = block_of(sums, dp, scaled_all, weight_line)
    received, share, input_grad = lax.optimization_barrier((received, share, input_grad))
    running = share[:token_rows].astype(wide) + from_core(share[token_rows:]).astype(wide)
    output = (running * col_scale[None, :]).astype(narrow)
    grad_sum = grads[0]
    for part in received:
        grad_sum += part.astype(wide)
    grad_factor = 1.0 / jnp.sqrt(jnp.float32(token_rows * dp_count))
    weight_grad = grad_sum * grad_factor
    return (output, input_grad, weight_grad)


def solution(mesh):
    placed = (P("dp", "tensor"), P("dp", "tensor"), P("dp", "tensor"), P())
    return jax.shard_map(
        on_device,
        mesh=mesh,
        in_specs=placed,
        out_specs=(P("dp", "tensor"), P("dp", "tensor"), P("dp", "tensor")),
        check_vma=False,
    )
```

```python
import jax
import jax.numpy as jnp
from jax import lax
from jax.experimental.layout import Layout, with_layout_constraint
from jax.sharding import PartitionSpec as P

BLOCK = 512
RING = 4
GROUPS = 16


def dp_of(x, z, core):
    return ((x % RING) * RING + z % RING) * 2 + core


def swap_pairs():
    return [
        (
            dp_of(y, z, core) * GROUPS + x * RING + low,
            dp_of(x, z, core) * GROUPS + y * RING + low,
        )
        for x in range(RING)
        for z in range(RING)
        for core in range(2)
        for y in range(RING)
        for low in range(RING)
    ]


def dp_pairs(dz, flip):
    return [
        (dp_of(x, z + dz, core ^ flip), dp_of(x, z, core))
        for x in range(RING)
        for z in range(RING)
        for core in range(2)
    ]


def groups_x():
    return [[dp_of(x, z, core) for x in range(RING)] for z in range(RING) for core in range(2)]


def groups_y():
    return [[y * RING + low for y in range(RING)] for low in range(RING)]


def groups_core_low():
    return [
        [
            dp_of(x, z, core) * GROUPS + y * RING + (z + i) % RING
            for i in range(RING)
            for core in range(2)
        ]
        for x in range(RING)
        for z in range(RING)
        for y in range(RING)
    ]


def from_core(block):
    return lax.ppermute(block, "dp", dp_pairs(0, 1))


def from_z(block, shift):
    return lax.ppermute(block, "dp", dp_pairs(shift, 0))


def swap(block):
    return lax.ppermute(block, ("dp", "tensor"), swap_pairs())


def row_major(array):
    return with_layout_constraint(array, Layout(major_to_minor=tuple(range(array.ndim))))


def exchange(parts, axis, groups):
    parts = row_major(parts)
    return row_major(lax.all_to_all(parts, axis, 0, 0, axis_index_groups=groups, tiled=True))


def collect(block, axis, groups):
    return exchange(jnp.broadcast_to(block[None], (len(groups[0]),) + block.shape), axis, groups)


def total(parts):
    return jnp.sum(parts.astype(jnp.float32), axis=0)


def block_of(steps, index, *operands):
    shapes = jax.eval_shape(steps, *operands)

    def nothing(*_):
        return jax.tree.map(lambda leaf: jnp.zeros(leaf.shape, leaf.dtype), shapes)

    return lax.cond(index >= 0, steps, nothing, *operands)


def near_first(pair, core):
    return jnp.where(core == 0, pair, pair[::-1])


def on_device(tokens, weight, cotangent, levels):
    token_rows, local_features = tokens.shape
    local_cols = weight.shape[1]
    half = local_features // 2
    dp_count = lax.axis_size("dp")
    dp = lax.axis_index("dp")
    core = dp % 2
    tensor = lax.axis_index("tensor")
    wide = jnp.float32
    narrow = jnp.bfloat16

    col_start = tensor * local_cols
    column_ids = col_start + jnp.arange(local_cols, dtype=jnp.int32)
    block_ids = column_ids // BLOCK
    block_range = jnp.arange(levels.shape[0], dtype=jnp.int32)
    membership = (block_ids[None, :] == block_range[:, None]).astype(wide)
    level_vals = levels.astype(wide) / 8.0
    col_scale = jnp.sum(membership * level_vals[:, None], axis=0)

    scaled = (cotangent.astype(wide) * col_scale[None, :]).astype(narrow)
    scaled_own = collect(scaled, "dp", groups_x())
    crossed = swap(tokens)
    scaled_all = jnp.stack([scaled_own, from_core(scaled_own)], axis=1).reshape(-1, local_cols)

    both = ("dp", "tensor")
    parts = jnp.stack([crossed[:, :half], crossed[:, half:]])
    parts = jnp.broadcast_to(parts[None], (RING, 2, token_rows, half))
    line = exchange(parts.reshape(2 * RING, token_rows, half), both, groups_core_low())
    line = line.reshape(RING, 2, token_rows, half)
    line = jnp.concatenate([line[i] for i in range(RING)], axis=2)
    line = near_first(line, core)
    line, weight = lax.optimization_barrier((line, weight))
    brick = collect(line, "tensor", groups_y()).reshape(-1, RING * half)

    weight_line = [weight] + [from_z(weight, i) for i in range(1, RING)]
    weight_line = jnp.concatenate(weight_line, axis=0)

    grads = lax.dot_general(brick, scaled_all, (((0,), (0,)), ((), ())), preferred_element_type=wide)
    grads = grads.reshape(RING, half, local_cols)
    away = [grads[i].astype(narrow) for i in range(1, RING)]
    received = [from_z(away[i - 1], -i) for i in range(1, RING)]

    def sums(scaled_all, brick, weight_line):
        term = lax.dot_general(scaled_all, weight_line, (((1,), (1,)), ((), ())), preferred_element_type=wide)
        term = row_major(term.astype(narrow)).reshape(RING, 2, token_rows, RING * half)
        term = near_first(total(exchange(term, "tensor", groups_y())).astype(narrow), core)
        term = jnp.stack([term[:, :, i * half:(i + 1) * half] for i in range(RING)])
        term = exchange(term.reshape(2 * RING, token_rows, half), both, groups_core_low())
        term = total(term.reshape(RING, 2, token_rows, half)).astype(narrow)
        input_grad = swap(jnp.concatenate([term[0], term[1]], axis=1))

        share = jnp.dot(brick, weight_line, preferred_element_type=wide)
        share = share.reshape(RING, 2, token_rows, local_cols)
        share = share[:, 0] + from_core(share[:, 1].astype(narrow)).astype(wide)
        running = total(exchange(share.astype(narrow), "dp", groups_x()))
        return running, input_grad

    running, input_grad = block_of(sums, dp, scaled_all, brick, weight_line)
    received, running, input_grad = lax.optimization_barrier((received, running, input_grad))
    output = (running * col_scale[None, :]).astype(narrow)
    grad_sum = grads[0]
    for part in received:
        grad_sum += part.astype(wide)
    grad_factor = 1.0 / jnp.sqrt(jnp.float32(token_rows * dp_count))
    weight_grad = grad_sum * grad_factor
    return (output, input_grad, weight_grad)


def solution(mesh):
    placed = (P("dp", "tensor"), P("dp", "tensor"), P("dp", "tensor"), P())
    return jax.shard_map(
        on_device,
        mesh=mesh,
        in_specs=placed,
        out_specs=(P("dp", "tensor"), P("dp", "tensor"), P("dp", "tensor")),
        check_vma=False,
    )
```

```python
import jax
import jax.numpy as jnp
from jax import lax
from jax.experimental.layout import Layout, with_layout_constraint
from jax.sharding import PartitionSpec as P

BLOCK = 512
RING = 4
GROUPS = 16


def dp_of(x, z, core):
    return ((x % RING) * RING + z % RING) * 2 + core


def swap_pairs():
    return [
        (
            dp_of(y, z, core) * GROUPS + x * RING + low,
            dp_of(x, z, core) * GROUPS + y * RING + low,
        )
        for x in range(RING)
        for z in range(RING)
        for core in range(2)
        for y in range(RING)
        for low in range(RING)
    ]


def dp_pairs(dz, flip):
    return [
        (dp_of(x, z + dz, core ^ flip), dp_of(x, z, core))
        for x in range(RING)
        for z in range(RING)
        for core in range(2)
    ]


def groups_x():
    return [[dp_of(x, z, core) for x in range(RING)] for z in range(RING) for core in range(2)]


def groups_z():
    return [[dp_of(x, z, core) for z in range(RING)] for x in range(RING) for core in range(2)]


def groups_y():
    return [[y * RING + low for y in range(RING)] for low in range(RING)]


def groups_core_low():
    return [
        [
            dp_of(x, z, core) * GROUPS + y * RING + low
            for low in range(RING)
            for core in range(2)
        ]
        for x in range(RING)
        for z in range(RING)
        for y in range(RING)
    ]


def from_core(block):
    return lax.ppermute(block, "dp", dp_pairs(0, 1))


def from_z(block, shift):
    return lax.ppermute(block, "dp", dp_pairs(shift, 0))


def swap(block):
    return lax.ppermute(block, ("dp", "tensor"), swap_pairs())


def row_major(array):
    return with_layout_constraint(array, Layout(major_to_minor=tuple(range(array.ndim))))


def exchange(parts, axis, groups):
    parts = row_major(parts)
    return row_major(lax.all_to_all(parts, axis, 0, 0, axis_index_groups=groups, tiled=True))


def collect(block, axis, groups):
    return exchange(jnp.broadcast_to(block[None], (len(groups[0]),) + block.shape), axis, groups)


def total(parts):
    return jnp.sum(parts.astype(jnp.float32), axis=0)


def block_of(steps, index, *operands):
    shapes = jax.eval_shape(steps, *operands)

    def nothing(*_):
        return jax.tree.map(lambda leaf: jnp.zeros(leaf.shape, leaf.dtype), shapes)

    return lax.cond(index >= 0, steps, nothing, *operands)


def near_first(pair, core):
    return jnp.where(core == 0, pair, pair[::-1])


def on_device(tokens, weight, cotangent, levels):
    token_rows, local_features = tokens.shape
    local_cols = weight.shape[1]
    half = local_features // 2
    dp_count = lax.axis_size("dp")
    dp = lax.axis_index("dp")
    core = dp % 2
    z_hi = (dp // 2) % RING
    tensor = lax.axis_index("tensor")
    wide = jnp.float32
    narrow = jnp.bfloat16

    col_start = tensor * local_cols
    column_ids = col_start + jnp.arange(local_cols, dtype=jnp.int32)
    block_ids = column_ids // BLOCK
    block_range = jnp.arange(levels.shape[0], dtype=jnp.int32)
    membership = (block_ids[None, :] == block_range[:, None]).astype(wide)
    level_vals = levels.astype(wide) / 8.0
    col_scale = jnp.sum(membership * level_vals[:, None], axis=0)

    scaled = (cotangent.astype(wide) * col_scale[None, :]).astype(narrow)
    scaled_pair = jnp.concatenate([scaled, from_core(scaled)], axis=0)
    scaled_pair, tokens = lax.optimization_barrier((scaled_pair, tokens))
    scaled_all = lax.all_gather(scaled_pair, "dp", axis=0, axis_index_groups=groups_x(), tiled=True)

    both = ("dp", "tensor")

    crossed = swap(tokens)
    parts = jnp.stack([crossed[:, :half], crossed[:, half:]])
    parts = jnp.broadcast_to(parts[None], (RING, 2, token_rows, half))
    line = exchange(parts.reshape(2 * RING, token_rows, half), both, groups_core_low())
    line = line.reshape(RING, 2, token_rows, half)
    line = jnp.concatenate([line[i] for i in range(RING)], axis=2)
    line = near_first(line, core)
    line, weight = lax.optimization_barrier((line, weight))
    brick = collect(line, "tensor", groups_y()).reshape(-1, RING * half)

    weight_line = lax.all_gather(weight, "dp", axis=0, axis_index_groups=groups_z(), tiled=True)
    brick, weight_line = lax.optimization_barrier((brick, weight_line))

    grads = lax.dot_general(brick, scaled_all, (((0,), (0,)), ((), ())), preferred_element_type=wide)
    grads = grads.reshape(RING, half, local_cols)
    at = [lax.dynamic_index_in_dim(grads, (z_hi + i) % RING, 0, keepdims=False) for i in range(RING)]
    away = [at[i].astype(narrow) for i in range(1, RING)]
    away, weight_line = lax.optimization_barrier((away, weight_line))
    received = [from_z(away[i - 1], -i) for i in range(1, RING)]

    share = jnp.dot(brick, weight_line, preferred_element_type=wide).astype(narrow)
    share, scaled_all = lax.optimization_barrier((share, scaled_all))
    share = lax.psum_scatter(
        share, "dp", scatter_dimension=0, axis_index_groups=groups_x(), tiled=True
    )

    def sums(scaled_all, weight_line):
        term = lax.dot_general(scaled_all, weight_line, (((1,), (1,)), ((), ())), preferred_element_type=wide)
        term = row_major(term.astype(narrow)).reshape(RING, 2, token_rows, RING * half)
        term = near_first(total(exchange(term, "tensor", groups_y())).astype(narrow), core)
        term = jnp.stack([term[:, :, i * half:(i + 1) * half] for i in range(RING)])
        term = exchange(term.reshape(2 * RING, token_rows, half), both, groups_core_low())
        term = total(term.reshape(RING, 2, token_rows, half)).astype(narrow)
        return swap(jnp.concatenate([term[0], term[1]], axis=1))

    input_grad = block_of(sums, dp, scaled_all, weight_line)
    received, share, input_grad = lax.optimization_barrier((received, share, input_grad))
    running = share[:token_rows].astype(wide) + from_core(share[token_rows:]).astype(wide)
    output = (running * col_scale[None, :]).astype(narrow)
    grad_sum = at[0]
    for part in received:
        grad_sum += part.astype(wide)
    grad_factor = 1.0 / jnp.sqrt(jnp.float32(token_rows * dp_count))
    weight_grad = grad_sum * grad_factor
    return (output, input_grad, weight_grad)


def solution(mesh):
    placed = (P("dp", "tensor"), P("dp", "tensor"), P("dp", "tensor"), P())
    return jax.shard_map(
        on_device,
        mesh=mesh,
        in_specs=placed,
        out_specs=(P("dp", "tensor"), P("dp", "tensor"), P("dp", "tensor")),
        check_vma=False,
    )
```

```python
import jax
import jax.numpy as jnp
from jax import lax
from jax.experimental.layout import Layout, with_layout_constraint
from jax.sharding import PartitionSpec as P

BLOCK = 512
RING = 4
GROUPS = 16


def dp_of(x, z, core):
    return ((x % RING) * RING + z % RING) * 2 + core


def swap_pairs():
    return [
        (
            dp_of(y, z, core) * GROUPS + x * RING + low,
            dp_of(x, z, core) * GROUPS + y * RING + low,
        )
        for x in range(RING)
        for z in range(RING)
        for core in range(2)
        for y in range(RING)
        for low in range(RING)
    ]


def core_pairs():
    return [
        (dp_of(x, z, core ^ 1), dp_of(x, z, core))
        for x in range(RING)
        for z in range(RING)
        for core in range(2)
    ]


def groups_x():
    return [[dp_of(x, z, core) for x in range(RING)] for z in range(RING) for core in range(2)]


def groups_z():
    return [[dp_of(x, z, core) for z in range(RING)] for x in range(RING) for core in range(2)]


def groups_y():
    return [[y * RING + low for y in range(RING)] for low in range(RING)]


def groups_core_low():
    return [
        [
            dp_of(x, z, core) * GROUPS + y * RING + low
            for low in range(RING)
            for core in range(2)
        ]
        for x in range(RING)
        for z in range(RING)
        for y in range(RING)
    ]


def from_core(block):
    return lax.ppermute(block, "dp", core_pairs())


def swap(block):
    return lax.ppermute(block, ("dp", "tensor"), swap_pairs())


def row_major(array):
    return with_layout_constraint(array, Layout(major_to_minor=tuple(range(array.ndim))))


def exchange(parts, axis, groups):
    parts = row_major(parts)
    return row_major(lax.all_to_all(parts, axis, 0, 0, axis_index_groups=groups, tiled=True))


def collect(block, axis, groups):
    return exchange(jnp.broadcast_to(block[None], (len(groups[0]),) + block.shape), axis, groups)


def total(parts):
    return jnp.sum(parts.astype(jnp.float32), axis=0)


def near_first(pair, core):
    return jnp.where(core == 0, pair, pair[::-1])


def on_device(tokens, weight, cotangent, levels):
    token_rows, local_features = tokens.shape
    local_cols = weight.shape[1]
    half = local_features // 2
    dp_count = lax.axis_size("dp")
    dp = lax.axis_index("dp")
    core = dp % 2
    tensor = lax.axis_index("tensor")
    wide = jnp.float32
    narrow = jnp.bfloat16

    col_start = tensor * local_cols
    column_ids = col_start + jnp.arange(local_cols, dtype=jnp.int32)
    block_ids = column_ids // BLOCK
    block_range = jnp.arange(levels.shape[0], dtype=jnp.int32)
    membership = (block_ids[None, :] == block_range[:, None]).astype(wide)
    level_vals = levels.astype(wide) / 8.0
    col_scale = jnp.sum(membership * level_vals[:, None], axis=0)

    scaled = (cotangent.astype(wide) * col_scale[None, :]).astype(narrow)
    scaled_pair = jnp.concatenate([scaled, from_core(scaled)], axis=0)
    scaled_pair, weight = lax.optimization_barrier((scaled_pair, weight))
    scaled_all = lax.all_gather(scaled_pair, "dp", axis=0, axis_index_groups=groups_x(), tiled=True)

    weight_line = lax.all_gather(weight, "dp", axis=0, axis_index_groups=groups_z(), tiled=True)

    both = ("dp", "tensor")
    crossed = swap(tokens)
    crossed, weight_line = lax.optimization_barrier((crossed, weight_line))
    parts = jnp.stack([crossed[:, :half], crossed[:, half:]])
    parts = jnp.broadcast_to(parts[None], (RING, 2, token_rows, half))
    line = exchange(parts.reshape(2 * RING, token_rows, half), both, groups_core_low())
    line = line.reshape(RING, 2, token_rows, half)
    line = jnp.concatenate([line[i] for i in range(RING)], axis=2)
    line = near_first(line, core)
    brick = collect(line, "tensor", groups_y()).reshape(-1, RING * half)

    term = lax.dot_general(scaled_all, weight_line, (((1,), (1,)), ((), ())), preferred_element_type=wide)
    term = row_major(term.astype(narrow)).reshape(RING, 2, token_rows, RING * half)
    term, brick = lax.optimization_barrier((term, brick))
    term = exchange(term, "tensor", groups_y())

    share = jnp.dot(brick, weight_line, preferred_element_type=wide).astype(narrow)
    share = lax.psum_scatter(
        share, "dp", scatter_dimension=0, axis_index_groups=groups_x(), tiled=True
    )

    grads = lax.dot_general(brick, scaled_all, (((0,), (0,)), ((), ())), preferred_element_type=wide)
    grads = lax.psum_scatter(
        grads.astype(narrow), "dp", scatter_dimension=0, axis_index_groups=groups_z(), tiled=True
    )
    grad_factor = 1.0 / jnp.sqrt(jnp.float32(token_rows * dp_count))
    weight_grad = grads.astype(wide) * grad_factor

    term, weight_grad = lax.optimization_barrier((term, weight_grad))
    term = near_first(total(term).astype(narrow), core)
    term = jnp.stack([term[:, :, i * half:(i + 1) * half] for i in range(RING)])
    term = exchange(term.reshape(2 * RING, token_rows, half), both, groups_core_low())
    term = total(term.reshape(RING, 2, token_rows, half)).astype(narrow)
    input_grad = swap(jnp.concatenate([term[0], term[1]], axis=1))

    running = share[:token_rows].astype(wide) + from_core(share[token_rows:]).astype(wide)
    output = (running * col_scale[None, :]).astype(narrow)
    return (output, input_grad, weight_grad)


def solution(mesh):
    placed = (P("dp", "tensor"), P("dp", "tensor"), P("dp", "tensor"), P())
    return jax.shard_map(
        on_device,
        mesh=mesh,
        in_specs=placed,
        out_specs=(P("dp", "tensor"), P("dp", "tensor"), P("dp", "tensor")),
        check_vma=False,
    )
```

```python
import jax
import jax.numpy as jnp
from jax import lax
from jax.experimental.layout import Layout, with_layout_constraint
from jax.sharding import PartitionSpec as P

BLOCK = 512
RING = 4
GROUPS = 16


def dp_of(x, z, core):
    return ((x % RING) * RING + z % RING) * 2 + core


def swap_pairs():
    return [
        (
            dp_of(y, z, core) * GROUPS + x * RING + low,
            dp_of(x, z, core) * GROUPS + y * RING + low,
        )
        for x in range(RING)
        for z in range(RING)
        for core in range(2)
        for y in range(RING)
        for low in range(RING)
    ]


def dp_pairs(dx, flip):
    return [
        (dp_of(x + dx, z, core ^ flip), dp_of(x, z, core))
        for x in range(RING)
        for z in range(RING)
        for core in range(2)
    ]


def groups_x():
    return [[dp_of(x, z, core) for x in range(RING)] for z in range(RING) for core in range(2)]


def groups_z():
    return [[dp_of(x, z, core) for z in range(RING)] for x in range(RING) for core in range(2)]


def groups_y():
    return [[y * RING + low for y in range(RING)] for low in range(RING)]


def groups_core_low():
    return [
        [
            dp_of(x, z, core) * GROUPS + y * RING + low
            for low in range(RING)
            for core in range(2)
        ]
        for x in range(RING)
        for z in range(RING)
        for y in range(RING)
    ]


def from_core(block):
    return lax.ppermute(block, "dp", dp_pairs(0, 1))


def from_x(block, shift):
    return lax.ppermute(block, "dp", dp_pairs(shift, 0))


def swap(block):
    return lax.ppermute(block, ("dp", "tensor"), swap_pairs())


def row_major(array):
    return with_layout_constraint(array, Layout(major_to_minor=tuple(range(array.ndim))))


def exchange(parts, axis, groups):
    parts = row_major(parts)
    return row_major(lax.all_to_all(parts, axis, 0, 0, axis_index_groups=groups, tiled=True))


def collect(block, axis, groups):
    return exchange(jnp.broadcast_to(block[None], (len(groups[0]),) + block.shape), axis, groups)


def total(parts):
    return jnp.sum(parts.astype(jnp.float32), axis=0)


def near_first(pair, core):
    return jnp.where(core == 0, pair, pair[::-1])


def on_device(tokens, weight, cotangent, levels):
    token_rows, local_features = tokens.shape
    local_cols = weight.shape[1]
    half = local_features // 2
    dp_count = lax.axis_size("dp")
    dp = lax.axis_index("dp")
    core = dp % 2
    x = dp // (2 * RING)
    tensor = lax.axis_index("tensor")
    wide = jnp.float32
    narrow = jnp.bfloat16

    col_start = tensor * local_cols
    column_ids = col_start + jnp.arange(local_cols, dtype=jnp.int32)
    block_ids = column_ids // BLOCK
    block_range = jnp.arange(levels.shape[0], dtype=jnp.int32)
    membership = (block_ids[None, :] == block_range[:, None]).astype(wide)
    level_vals = levels.astype(wide) / 8.0
    col_scale = jnp.sum(membership * level_vals[:, None], axis=0)

    scaled = (cotangent.astype(wide) * col_scale[None, :]).astype(narrow)
    scaled_pair = jnp.concatenate([scaled, from_core(scaled)], axis=0)
    scaled_pair, tokens = lax.optimization_barrier((scaled_pair, tokens))
    scaled_all = lax.all_gather(scaled_pair, "dp", axis=0, axis_index_groups=groups_x(), tiled=True)

    both = ("dp", "tensor")

    crossed = swap(tokens)
    parts = jnp.stack([crossed[:, :half], crossed[:, half:]])
    parts = jnp.broadcast_to(parts[None], (RING, 2, token_rows, half))
    line = exchange(parts.reshape(2 * RING, token_rows, half), both, groups_core_low())
    line = line.reshape(RING, 2, token_rows, half)
    line = jnp.concatenate([line[i] for i in range(RING)], axis=2)
    line = near_first(line, core)
    line, weight = lax.optimization_barrier((line, weight))
    brick = collect(line, "tensor", groups_y()).reshape(-1, RING * half)

    weight_line = lax.all_gather(weight, "dp", axis=0, axis_index_groups=groups_z(), tiled=True)
    brick, weight_line = lax.optimization_barrier((brick, weight_line))

    grads = lax.dot_general(brick, scaled_all, (((0,), (0,)), ((), ())), preferred_element_type=wide)
    grads = grads.astype(narrow)
    grads, brick, weight_line = lax.optimization_barrier((grads, brick, weight_line))
    grads = lax.psum_scatter(
        grads, "dp", scatter_dimension=0, axis_index_groups=groups_z(), tiled=True
    )
    grad_factor = 1.0 / jnp.sqrt(jnp.float32(token_rows * dp_count))
    weight_grad = grads.astype(wide) * grad_factor

    term = lax.dot_general(scaled_all, weight_line, (((1,), (1,)), ((), ())), preferred_element_type=wide)
    term = row_major(term.astype(narrow)).reshape(RING, 2, token_rows, RING * half)
    term = near_first(total(exchange(term, "tensor", groups_y())).astype(narrow), core)
    term = jnp.stack([term[:, :, i * half:(i + 1) * half] for i in range(RING)])

    share = jnp.dot(brick, weight_line, preferred_element_type=wide)
    share = share.reshape(RING, 2, token_rows, local_cols)
    other = from_core(share[:, 1].astype(narrow))
    pieces = []
    for i in range(RING):
        at = (x + i) % RING
        piece = lax.dynamic_index_in_dim(share[:, 0], at, 0, keepdims=False)
        pieces.append(piece + lax.dynamic_index_in_dim(other, at, 0, keepdims=False).astype(wide))
    near = pieces[0]
    away = [piece.astype(narrow) for piece in pieces[1:]]
    away, term = lax.optimization_barrier((away, term))
    running = near
    for i in range(1, RING):
        running += from_x(away[i - 1], -i).astype(wide)

    term = exchange(term.reshape(2 * RING, token_rows, half), both, groups_core_low())
    term = total(term.reshape(RING, 2, token_rows, half)).astype(narrow)
    input_grad = swap(jnp.concatenate([term[0], term[1]], axis=1))

    output = (running * col_scale[None, :]).astype(narrow)
    return (output, input_grad, weight_grad)


def solution(mesh):
    placed = (P("dp", "tensor"), P("dp", "tensor"), P("dp", "tensor"), P())
    return jax.shard_map(
        on_device,
        mesh=mesh,
        in_specs=placed,
        out_specs=(P("dp", "tensor"), P("dp", "tensor"), P("dp", "tensor")),
        check_vma=False,
    )
```

```python
import jax
import jax.numpy as jnp
from jax import lax
from jax.experimental.layout import Layout, with_layout_constraint
from jax.sharding import PartitionSpec as P

BLOCK = 512
RING = 4
GROUPS = 16


def dp_of(x, z, core):
    return ((x % RING) * RING + z % RING) * 2 + core


def swap_pairs():
    return [
        (
            dp_of(y, z, core) * GROUPS + x * RING + low,
            dp_of(x, z, core) * GROUPS + y * RING + low,
        )
        for x in range(RING)
        for z in range(RING)
        for core in range(2)
        for y in range(RING)
        for low in range(RING)
    ]


def dp_pairs(dx, flip):
    return [
        (dp_of(x + dx, z, core ^ flip), dp_of(x, z, core))
        for x in range(RING)
        for z in range(RING)
        for core in range(2)
    ]


def groups_x():
    return [[dp_of(x, z, core) for x in range(RING)] for z in range(RING) for core in range(2)]


def groups_z():
    return [[dp_of(x, z, core) for z in range(RING)] for x in range(RING) for core in range(2)]


def groups_y():
    return [[y * RING + low for y in range(RING)] for low in range(RING)]


def groups_core_low():
    return [
        [
            dp_of(x, z, core) * GROUPS + y * RING + low
            for low in range(RING)
            for core in range(2)
        ]
        for x in range(RING)
        for z in range(RING)
        for y in range(RING)
    ]


def from_core(block):
    return lax.ppermute(block, "dp", dp_pairs(0, 1))


def from_x(block, shift):
    return lax.ppermute(block, "dp", dp_pairs(shift, 0))


def swap(block):
    return lax.ppermute(block, ("dp", "tensor"), swap_pairs())


def row_major(array):
    return with_layout_constraint(array, Layout(major_to_minor=tuple(range(array.ndim))))


def exchange(parts, axis, groups):
    parts = row_major(parts)
    return row_major(lax.all_to_all(parts, axis, 0, 0, axis_index_groups=groups, tiled=True))


def collect(block, axis, groups):
    return exchange(jnp.broadcast_to(block[None], (len(groups[0]),) + block.shape), axis, groups)


def total(parts):
    return jnp.sum(parts.astype(jnp.float32), axis=0)


def block_of(steps, index, *operands):
    shapes = jax.eval_shape(steps, *operands)

    def nothing(*_):
        return jax.tree.map(lambda leaf: jnp.zeros(leaf.shape, leaf.dtype), shapes)

    return lax.cond(index >= 0, steps, nothing, *operands)


def near_first(pair, core):
    return jnp.where(core == 0, pair, pair[::-1])


def on_device(tokens, weight, cotangent, levels):
    token_rows, local_features = tokens.shape
    local_cols = weight.shape[1]
    half = local_features // 2
    dp_count = lax.axis_size("dp")
    dp = lax.axis_index("dp")
    core = dp % 2
    x = dp // (2 * RING)
    tensor = lax.axis_index("tensor")
    wide = jnp.float32
    narrow = jnp.bfloat16

    col_start = tensor * local_cols
    column_ids = col_start + jnp.arange(local_cols, dtype=jnp.int32)
    block_ids = column_ids // BLOCK
    block_range = jnp.arange(levels.shape[0], dtype=jnp.int32)
    membership = (block_ids[None, :] == block_range[:, None]).astype(wide)
    level_vals = levels.astype(wide) / 8.0
    col_scale = jnp.sum(membership * level_vals[:, None], axis=0)

    scaled = (cotangent.astype(wide) * col_scale[None, :]).astype(narrow)
    scaled_pair = jnp.concatenate([scaled, from_core(scaled)], axis=0)
    scaled_pair, tokens = lax.optimization_barrier((scaled_pair, tokens))
    scaled_all = lax.all_gather(scaled_pair, "dp", axis=0, axis_index_groups=groups_x(), tiled=True)

    both = ("dp", "tensor")

    crossed = swap(tokens)
    parts = jnp.stack([crossed[:, :half], crossed[:, half:]])
    parts = jnp.broadcast_to(parts[None], (RING, 2, token_rows, half))
    line = exchange(parts.reshape(2 * RING, token_rows, half), both, groups_core_low())
    line = line.reshape(RING, 2, token_rows, half)
    line = jnp.concatenate([line[i] for i in range(RING)], axis=2)
    line = near_first(line, core)
    line, weight = lax.optimization_barrier((line, weight))
    brick = collect(line, "tensor", groups_y()).reshape(-1, RING * half)

    weight_line = lax.all_gather(weight, "dp", axis=0, axis_index_groups=groups_z(), tiled=True)
    brick, weight_line = lax.optimization_barrier((brick, weight_line))

    grads = lax.dot_general(brick, scaled_all, (((0,), (0,)), ((), ())), preferred_element_type=wide)
    grads = grads.astype(narrow)
    grads, brick, weight_line = lax.optimization_barrier((grads, brick, weight_line))
    grads = lax.psum_scatter(
        grads, "dp", scatter_dimension=0, axis_index_groups=groups_z(), tiled=True
    )
    grad_factor = 1.0 / jnp.sqrt(jnp.float32(token_rows * dp_count))
    weight_grad = grads.astype(wide) * grad_factor

    def sums(scaled_all, brick, weight_line):
        term = lax.dot_general(scaled_all, weight_line, (((1,), (1,)), ((), ())), preferred_element_type=wide)
        term = row_major(term.astype(narrow)).reshape(RING, 2, token_rows, RING * half)
        term = near_first(total(exchange(term, "tensor", groups_y())).astype(narrow), core)
        term = jnp.stack([term[:, :, i * half:(i + 1) * half] for i in range(RING)])

        share = jnp.dot(brick, weight_line, preferred_element_type=wide)
        share = share.reshape(RING, 2, token_rows, local_cols)
        other = from_core(share[:, 1].astype(narrow))
        pieces = []
        for i in range(RING):
            at = (x + i) % RING
            piece = lax.dynamic_index_in_dim(share[:, 0], at, 0, keepdims=False)
            pieces.append(piece + lax.dynamic_index_in_dim(other, at, 0, keepdims=False).astype(wide))
        near = pieces[0]
        away = [piece.astype(narrow) for piece in pieces[1:]]
        away, term = lax.optimization_barrier((away, term))
        running = near
        for i in range(1, RING):
            running += from_x(away[i - 1], -i).astype(wide)

        term = exchange(term.reshape(2 * RING, token_rows, half), both, groups_core_low())
        term = total(term.reshape(RING, 2, token_rows, half)).astype(narrow)
        input_grad = swap(jnp.concatenate([term[0], term[1]], axis=1))
        return running, input_grad

    running, input_grad = block_of(sums, dp, scaled_all, brick, weight_line)
    output = (running * col_scale[None, :]).astype(narrow)
    return (output, input_grad, weight_grad)


def solution(mesh):
    placed = (P("dp", "tensor"), P("dp", "tensor"), P("dp", "tensor"), P())
    return jax.shard_map(
        on_device,
        mesh=mesh,
        in_specs=placed,
        out_specs=(P("dp", "tensor"), P("dp", "tensor"), P("dp", "tensor")),
        check_vma=False,
    )
```

```python
import jax
import jax.numpy as jnp
from jax import lax
from jax.experimental.layout import Layout, with_layout_constraint
from jax.sharding import PartitionSpec as P

BLOCK = 512
RING = 4
GROUPS = 16


def dp_of(x, z, core):
    return ((x % RING) * RING + z % RING) * 2 + core


def swap_pairs():
    return [
        (
            dp_of(y, z, core) * GROUPS + x * RING + low,
            dp_of(x, z, core) * GROUPS + y * RING + low,
        )
        for x in range(RING)
        for z in range(RING)
        for core in range(2)
        for y in range(RING)
        for low in range(RING)
    ]


def dp_pairs(dx, flip):
    return [
        (dp_of(x + dx, z, core ^ flip), dp_of(x, z, core))
        for x in range(RING)
        for z in range(RING)
        for core in range(2)
    ]


def groups_x():
    return [[dp_of(x, z, core) for x in range(RING)] for z in range(RING) for core in range(2)]


def groups_z():
    return [[dp_of(x, z, core) for z in range(RING)] for x in range(RING) for core in range(2)]


def groups_y():
    return [[y * RING + low for y in range(RING)] for low in range(RING)]


def groups_core_low():
    return [
        [
            dp_of(x, z, core) * GROUPS + y * RING + low
            for low in range(RING)
            for core in range(2)
        ]
        for x in range(RING)
        for z in range(RING)
        for y in range(RING)
    ]


def from_core(block):
    return lax.ppermute(block, "dp", dp_pairs(0, 1))


def from_x(block, shift):
    return lax.ppermute(block, "dp", dp_pairs(shift, 0))


def swap(block):
    return lax.ppermute(block, ("dp", "tensor"), swap_pairs())


def row_major(array):
    return with_layout_constraint(array, Layout(major_to_minor=tuple(range(array.ndim))))


def exchange(parts, axis, groups):
    parts = row_major(parts)
    return row_major(lax.all_to_all(parts, axis, 0, 0, axis_index_groups=groups, tiled=True))


def collect(block, axis, groups):
    return exchange(jnp.broadcast_to(block[None], (len(groups[0]),) + block.shape), axis, groups)


def total(parts):
    return jnp.sum(parts.astype(jnp.float32), axis=0)


def block_of(steps, index, *operands):
    shapes = jax.eval_shape(steps, *operands)

    def nothing(*_):
        return jax.tree.map(lambda leaf: jnp.zeros(leaf.shape, leaf.dtype), shapes)

    return lax.cond(index >= 0, steps, nothing, *operands)


def near_first(pair, core):
    return jnp.where(core == 0, pair, pair[::-1])


def on_device(tokens, weight, cotangent, levels):
    token_rows, local_features = tokens.shape
    local_cols = weight.shape[1]
    half = local_features // 2
    dp_count = lax.axis_size("dp")
    dp = lax.axis_index("dp")
    core = dp % 2
    x = dp // (2 * RING)
    tensor = lax.axis_index("tensor")
    wide = jnp.float32
    narrow = jnp.bfloat16

    col_start = tensor * local_cols
    column_ids = col_start + jnp.arange(local_cols, dtype=jnp.int32)
    block_ids = column_ids // BLOCK
    block_range = jnp.arange(levels.shape[0], dtype=jnp.int32)
    membership = (block_ids[None, :] == block_range[:, None]).astype(wide)
    level_vals = levels.astype(wide) / 8.0
    col_scale = jnp.sum(membership * level_vals[:, None], axis=0)

    scaled = (cotangent.astype(wide) * col_scale[None, :]).astype(narrow)
    both = ("dp", "tensor")
    scaled_pair = jnp.concatenate([scaled, from_core(scaled)], axis=0)

    crossed = swap(tokens)
    parts = jnp.stack([crossed[:, :half], crossed[:, half:]])
    parts = jnp.broadcast_to(parts[None], (RING, 2, token_rows, half))
    line = exchange(parts.reshape(2 * RING, token_rows, half), both, groups_core_low())
    line = line.reshape(RING, 2, token_rows, half)
    line = jnp.concatenate([line[i] for i in range(RING)], axis=2)
    line = near_first(line, core)
    line, weight, scaled_pair = lax.optimization_barrier((line, weight, scaled_pair))
    brick = collect(line, "tensor", groups_y()).reshape(-1, RING * half)

    scaled_all = lax.all_gather(scaled_pair, "dp", axis=0, axis_index_groups=groups_x(), tiled=True)

    weight_line = lax.all_gather(weight, "dp", axis=0, axis_index_groups=groups_z(), tiled=True)
    brick, weight_line = lax.optimization_barrier((brick, weight_line))

    grads = lax.dot_general(brick, scaled_all, (((0,), (0,)), ((), ())), preferred_element_type=wide)
    grads = grads.astype(narrow)
    grads, brick, weight_line = lax.optimization_barrier((grads, brick, weight_line))
    grads = lax.psum_scatter(
        grads, "dp", scatter_dimension=0, axis_index_groups=groups_z(), tiled=True
    )
    grad_factor = 1.0 / jnp.sqrt(jnp.float32(token_rows * dp_count))
    weight_grad = grads.astype(wide) * grad_factor

    def sums(scaled_all, brick, weight_line):
        term = lax.dot_general(scaled_all, weight_line, (((1,), (1,)), ((), ())), preferred_element_type=wide)
        term = row_major(term.astype(narrow)).reshape(RING, 2, token_rows, RING * half)
        term = near_first(total(exchange(term, "tensor", groups_y())).astype(narrow), core)
        term = jnp.stack([term[:, :, i * half:(i + 1) * half] for i in range(RING)])

        share = jnp.dot(brick, weight_line, preferred_element_type=wide)
        share = share.reshape(RING, 2, token_rows, local_cols)
        other = from_core(share[:, 1].astype(narrow))
        pieces = []
        for i in range(RING):
            at = (x + i) % RING
            piece = lax.dynamic_index_in_dim(share[:, 0], at, 0, keepdims=False)
            pieces.append(piece + lax.dynamic_index_in_dim(other, at, 0, keepdims=False).astype(wide))
        near = pieces[0]
        away = [piece.astype(narrow) for piece in pieces[1:]]
        away, term = lax.optimization_barrier((away, term))
        running = near
        for i in range(1, RING):
            running += from_x(away[i - 1], -i).astype(wide)

        term = exchange(term.reshape(2 * RING, token_rows, half), both, groups_core_low())
        term = total(term.reshape(RING, 2, token_rows, half)).astype(narrow)
        input_grad = swap(jnp.concatenate([term[0], term[1]], axis=1))
        return running, input_grad

    running, input_grad = block_of(sums, dp, scaled_all, brick, weight_line)
    output = (running * col_scale[None, :]).astype(narrow)
    return (output, input_grad, weight_grad)


def solution(mesh):
    placed = (P("dp", "tensor"), P("dp", "tensor"), P("dp", "tensor"), P())
    return jax.shard_map(
        on_device,
        mesh=mesh,
        in_specs=placed,
        out_specs=(P("dp", "tensor"), P("dp", "tensor"), P("dp", "tensor")),
        check_vma=False,
    )
```

```python
import jax
import jax.numpy as jnp
from jax import lax
from jax.experimental.layout import Layout, with_layout_constraint
from jax.sharding import PartitionSpec as P

BLOCK = 512
RING = 4
GROUPS = 16


def dp_of(x, z, core):
    return ((x % RING) * RING + z % RING) * 2 + core


def swap_pairs():
    return [
        (
            dp_of(y, z, core) * GROUPS + x * RING + low,
            dp_of(x, z, core) * GROUPS + y * RING + low,
        )
        for x in range(RING)
        for z in range(RING)
        for core in range(2)
        for y in range(RING)
        for low in range(RING)
    ]


def dp_pairs(dx, flip):
    return [
        (dp_of(x + dx, z, core ^ flip), dp_of(x, z, core))
        for x in range(RING)
        for z in range(RING)
        for core in range(2)
    ]


def groups_x():
    return [[dp_of(x, z, core) for x in range(RING)] for z in range(RING) for core in range(2)]


def groups_z():
    return [[dp_of(x, z, core) for z in range(RING)] for x in range(RING) for core in range(2)]


def groups_y():
    return [[y * RING + low for y in range(RING)] for low in range(RING)]


def groups_core_low():
    return [
        [
            dp_of(x, z, core) * GROUPS + y * RING + low
            for low in range(RING)
            for core in range(2)
        ]
        for x in range(RING)
        for z in range(RING)
        for y in range(RING)
    ]


def from_core(block):
    return lax.ppermute(block, "dp", dp_pairs(0, 1))


def from_x(block, shift):
    return lax.ppermute(block, "dp", dp_pairs(shift, 0))


def swap(block):
    return lax.ppermute(block, ("dp", "tensor"), swap_pairs())


def row_major(array):
    return with_layout_constraint(array, Layout(major_to_minor=tuple(range(array.ndim))))


def exchange(parts, axis, groups):
    parts = row_major(parts)
    return row_major(lax.all_to_all(parts, axis, 0, 0, axis_index_groups=groups, tiled=True))


def collect(block, axis, groups):
    return exchange(jnp.broadcast_to(block[None], (len(groups[0]),) + block.shape), axis, groups)


def total(parts):
    return jnp.sum(parts.astype(jnp.float32), axis=0)


def block_of(steps, index, *operands):
    shapes = jax.eval_shape(steps, *operands)

    def nothing(*_):
        return jax.tree.map(lambda leaf: jnp.zeros(leaf.shape, leaf.dtype), shapes)

    return lax.cond(index >= 0, steps, nothing, *operands)


def near_first(pair, core):
    return jnp.where(core == 0, pair, pair[::-1])


def on_device(tokens, weight, cotangent, levels):
    token_rows, local_features = tokens.shape
    local_cols = weight.shape[1]
    half = local_features // 2
    dp_count = lax.axis_size("dp")
    dp = lax.axis_index("dp")
    core = dp % 2
    x = dp // (2 * RING)
    tensor = lax.axis_index("tensor")
    wide = jnp.float32
    narrow = jnp.bfloat16

    col_start = tensor * local_cols
    column_ids = col_start + jnp.arange(local_cols, dtype=jnp.int32)
    block_ids = column_ids // BLOCK
    block_range = jnp.arange(levels.shape[0], dtype=jnp.int32)
    membership = (block_ids[None, :] == block_range[:, None]).astype(wide)
    level_vals = levels.astype(wide) / 8.0
    col_scale = jnp.sum(membership * level_vals[:, None], axis=0)

    scaled = (cotangent.astype(wide) * col_scale[None, :]).astype(narrow)
    both = ("dp", "tensor")
    scaled_pair = jnp.concatenate([scaled, from_core(scaled)], axis=0)

    crossed, weight, scaled_pair = lax.optimization_barrier((swap(tokens), weight, scaled_pair))

    scaled_all = lax.all_gather(scaled_pair, "dp", axis=0, axis_index_groups=groups_x(), tiled=True)

    weight_line = lax.all_gather(weight, "dp", axis=0, axis_index_groups=groups_z(), tiled=True)

    parts = jnp.stack([crossed[:, :half], crossed[:, half:]])
    parts = jnp.broadcast_to(parts[None], (RING, 2, token_rows, half))
    line = exchange(parts.reshape(2 * RING, token_rows, half), both, groups_core_low())
    line, weight_line = lax.optimization_barrier((line, weight_line))
    line = line.reshape(RING, 2, token_rows, half)
    line = jnp.concatenate([line[i] for i in range(RING)], axis=2)
    line = near_first(line, core)
    brick = collect(line, "tensor", groups_y()).reshape(-1, RING * half)

    term = lax.dot_general(scaled_all, weight_line, (((1,), (1,)), ((), ())), preferred_element_type=wide)
    term = row_major(term.astype(narrow)).reshape(RING, 2, token_rows, RING * half)
    term, brick = lax.optimization_barrier((term, brick))

    grads = lax.dot_general(brick, scaled_all, (((0,), (0,)), ((), ())), preferred_element_type=wide)
    grads = grads.astype(narrow)
    grads, brick, weight_line = lax.optimization_barrier((grads, brick, weight_line))
    grads = lax.psum_scatter(
        grads, "dp", scatter_dimension=0, axis_index_groups=groups_z(), tiled=True
    )
    grad_factor = 1.0 / jnp.sqrt(jnp.float32(token_rows * dp_count))
    weight_grad = grads.astype(wide) * grad_factor

    def sums(term, brick, weight_line):
        term = near_first(total(exchange(term, "tensor", groups_y())).astype(narrow), core)
        term = jnp.stack([term[:, :, i * half:(i + 1) * half] for i in range(RING)])

        share = jnp.dot(brick, weight_line, preferred_element_type=wide)
        share = share.reshape(RING, 2, token_rows, local_cols)
        other = from_core(share[:, 1].astype(narrow))
        pieces = []
        for i in range(RING):
            at = (x + i) % RING
            piece = lax.dynamic_index_in_dim(share[:, 0], at, 0, keepdims=False)
            pieces.append(piece + lax.dynamic_index_in_dim(other, at, 0, keepdims=False).astype(wide))
        near = pieces[0]
        away = [piece.astype(narrow) for piece in pieces[1:]]
        away, term = lax.optimization_barrier((away, term))
        running = near
        for i in range(1, RING):
            running += from_x(away[i - 1], -i).astype(wide)

        term = exchange(term.reshape(2 * RING, token_rows, half), both, groups_core_low())
        term = total(term.reshape(RING, 2, token_rows, half)).astype(narrow)
        input_grad = swap(jnp.concatenate([term[0], term[1]], axis=1))
        return running, input_grad

    running, input_grad = block_of(sums, dp, term, brick, weight_line)
    output = (running * col_scale[None, :]).astype(narrow)
    return (output, input_grad, weight_grad)


def solution(mesh):
    placed = (P("dp", "tensor"), P("dp", "tensor"), P("dp", "tensor"), P())
    return jax.shard_map(
        on_device,
        mesh=mesh,
        in_specs=placed,
        out_specs=(P("dp", "tensor"), P("dp", "tensor"), P("dp", "tensor")),
        check_vma=False,
    )
```

```python
import jax
import jax.numpy as jnp
from jax import lax
from jax.experimental.layout import Layout, with_layout_constraint
from jax.sharding import PartitionSpec as P

BLOCK = 512
RING = 4
GROUPS = 16


def dp_of(x, z, core):
    return ((x % RING) * RING + z % RING) * 2 + core


def swap_pairs():
    return [
        (
            dp_of(y, z, core) * GROUPS + x * RING + low,
            dp_of(x, z, core) * GROUPS + y * RING + low,
        )
        for x in range(RING)
        for z in range(RING)
        for core in range(2)
        for y in range(RING)
        for low in range(RING)
    ]


def dp_pairs(dx, flip):
    return [
        (dp_of(x + dx, z, core ^ flip), dp_of(x, z, core))
        for x in range(RING)
        for z in range(RING)
        for core in range(2)
    ]


def groups_x():
    return [[dp_of(x, z, core) for x in range(RING)] for z in range(RING) for core in range(2)]


def groups_z():
    return [[dp_of(x, z, core) for z in range(RING)] for x in range(RING) for core in range(2)]


def groups_y():
    return [[y * RING + low for y in range(RING)] for low in range(RING)]


def groups_core_low():
    return [
        [
            dp_of(x, z, core) * GROUPS + y * RING + low
            for low in range(RING)
            for core in range(2)
        ]
        for x in range(RING)
        for z in range(RING)
        for y in range(RING)
    ]


def from_core(block):
    return lax.ppermute(block, "dp", dp_pairs(0, 1))


def from_x(block, shift):
    return lax.ppermute(block, "dp", dp_pairs(shift, 0))


def swap(block):
    return lax.ppermute(block, ("dp", "tensor"), swap_pairs())


def row_major(array):
    return with_layout_constraint(array, Layout(major_to_minor=tuple(range(array.ndim))))


def exchange(parts, axis, groups):
    parts = row_major(parts)
    return row_major(lax.all_to_all(parts, axis, 0, 0, axis_index_groups=groups, tiled=True))


def collect(block, axis, groups):
    return exchange(jnp.broadcast_to(block[None], (len(groups[0]),) + block.shape), axis, groups)


def total(parts):
    return jnp.sum(parts.astype(jnp.float32), axis=0)


def block_of(steps, index, *operands):
    shapes = jax.eval_shape(steps, *operands)

    def nothing(*_):
        return jax.tree.map(lambda leaf: jnp.zeros(leaf.shape, leaf.dtype), shapes)

    return lax.cond(index >= 0, steps, nothing, *operands)


def near_first(pair, core):
    return jnp.where(core == 0, pair, pair[::-1])


def on_device(tokens, weight, cotangent, levels):
    token_rows, local_features = tokens.shape
    local_cols = weight.shape[1]
    half = local_features // 2
    dp_count = lax.axis_size("dp")
    dp = lax.axis_index("dp")
    core = dp % 2
    x = dp // (2 * RING)
    tensor = lax.axis_index("tensor")
    wide = jnp.float32
    narrow = jnp.bfloat16

    col_start = tensor * local_cols
    column_ids = col_start + jnp.arange(local_cols, dtype=jnp.int32)
    block_ids = column_ids // BLOCK
    block_range = jnp.arange(levels.shape[0], dtype=jnp.int32)
    membership = (block_ids[None, :] == block_range[:, None]).astype(wide)
    level_vals = levels.astype(wide) / 8.0
    col_scale = jnp.sum(membership * level_vals[:, None], axis=0)

    scaled = (cotangent.astype(wide) * col_scale[None, :]).astype(narrow)
    both = ("dp", "tensor")
    scaled_pair = jnp.concatenate([scaled, from_core(scaled)], axis=0)

    crossed = swap(tokens)
    parts = jnp.stack([crossed[:, :half], crossed[:, half:]])
    parts = jnp.broadcast_to(parts[None], (RING, 2, token_rows, half))
    line = exchange(parts.reshape(2 * RING, token_rows, half), both, groups_core_low())
    line = line.reshape(RING, 2, token_rows, half)
    line = jnp.concatenate([line[i] for i in range(RING)], axis=2)
    line = near_first(line, core)
    line, weight, scaled_pair = lax.optimization_barrier((line, weight, scaled_pair))
    brick = collect(line, "tensor", groups_y()).reshape(-1, RING * half)

    scaled_all = lax.all_gather(scaled_pair, "dp", axis=0, axis_index_groups=groups_x(), tiled=True)

    weight_line = lax.all_gather(weight, "dp", axis=0, axis_index_groups=groups_z(), tiled=True)
    brick, weight_line = lax.optimization_barrier((brick, weight_line))

    grads = lax.dot_general(brick, scaled_all, (((0,), (0,)), ((), ())), preferred_element_type=wide)
    grads = grads.astype(narrow)
    grads, brick, weight_line = lax.optimization_barrier((grads, brick, weight_line))
    grads = lax.psum_scatter(
        grads, "dp", scatter_dimension=0, axis_index_groups=groups_z(), tiled=True
    )
    grad_factor = 1.0 / jnp.sqrt(jnp.float32(token_rows * dp_count))
    weight_grad = grads.astype(wide) * grad_factor

    def sums(scaled_all, brick, weight_line):
        term = lax.dot_general(scaled_all, weight_line, (((1,), (1,)), ((), ())), preferred_element_type=wide)
        term = row_major(term.astype(narrow)).reshape(RING, 2, token_rows, RING * half)
        term = near_first(total(exchange(term, "tensor", groups_y())).astype(narrow), core)
        term = jnp.stack([term[:, :, i * half:(i + 1) * half] for i in range(RING)])

        share = jnp.dot(brick, weight_line, preferred_element_type=wide)
        share = share.reshape(RING, 2, token_rows, local_cols)
        other = from_core(share[:, 1].astype(narrow))
        pieces = []
        for i in range(RING):
            at = (x + i) % RING
            piece = lax.dynamic_index_in_dim(share[:, 0], at, 0, keepdims=False)
            pieces.append(piece + lax.dynamic_index_in_dim(other, at, 0, keepdims=False).astype(wide))
        near = pieces[0]
        away = [piece.astype(narrow) for piece in pieces[1:]]
        away, term = lax.optimization_barrier((away, term))
        running = near
        for i in range(1, RING):
            running += from_x(away[i - 1], -i).astype(wide)

        term = swap(term.reshape(2 * RING, token_rows, half))
        term = exchange(term, both, groups_core_low())
        term = total(term.reshape(RING, 2, token_rows, half)).astype(narrow)
        input_grad = jnp.concatenate([term[0], term[1]], axis=1)
        return running, input_grad

    running, input_grad = block_of(sums, dp, scaled_all, brick, weight_line)
    output = (running * col_scale[None, :]).astype(narrow)
    return (output, input_grad, weight_grad)


def solution(mesh):
    placed = (P("dp", "tensor"), P("dp", "tensor"), P("dp", "tensor"), P())
    return jax.shard_map(
        on_device,
        mesh=mesh,
        in_specs=placed,
        out_specs=(P("dp", "tensor"), P("dp", "tensor"), P("dp", "tensor")),
        check_vma=False,
    )
```

```python
import jax
import jax.numpy as jnp
from jax import lax
from jax.experimental.layout import Layout, with_layout_constraint
from jax.sharding import PartitionSpec as P

BLOCK = 512
RING = 4
GROUPS = 16


def dp_of(x, z, core):
    return ((x % RING) * RING + z % RING) * 2 + core


def swap_pairs():
    return [
        (
            dp_of(y, z, core) * GROUPS + x * RING + low,
            dp_of(x, z, core) * GROUPS + y * RING + low,
        )
        for x in range(RING)
        for z in range(RING)
        for core in range(2)
        for y in range(RING)
        for low in range(RING)
    ]


def dp_pairs(dx, flip):
    return [
        (dp_of(x + dx, z, core ^ flip), dp_of(x, z, core))
        for x in range(RING)
        for z in range(RING)
        for core in range(2)
    ]


def groups_x():
    return [[dp_of(x, z, core) for x in range(RING)] for z in range(RING) for core in range(2)]


def groups_z():
    return [[dp_of(x, z, core) for z in range(RING)] for x in range(RING) for core in range(2)]


def groups_y():
    return [[y * RING + low for y in range(RING)] for low in range(RING)]


def groups_core_low():
    return [
        [
            dp_of(x, z, core) * GROUPS + y * RING + low
            for low in range(RING)
            for core in range(2)
        ]
        for x in range(RING)
        for z in range(RING)
        for y in range(RING)
    ]


def from_core(block):
    return lax.ppermute(block, "dp", dp_pairs(0, 1))


def from_x(block, shift):
    return lax.ppermute(block, "dp", dp_pairs(shift, 0))


def swap(block):
    return lax.ppermute(block, ("dp", "tensor"), swap_pairs())


def row_major(array):
    return with_layout_constraint(array, Layout(major_to_minor=tuple(range(array.ndim))))


def exchange(parts, axis, groups):
    parts = row_major(parts)
    return row_major(lax.all_to_all(parts, axis, 0, 0, axis_index_groups=groups, tiled=True))


def collect(block, axis, groups):
    return exchange(jnp.broadcast_to(block[None], (len(groups[0]),) + block.shape), axis, groups)


def total(parts):
    return jnp.sum(parts.astype(jnp.float32), axis=0)


def block_of(steps, index, *operands):
    shapes = jax.eval_shape(steps, *operands)

    def nothing(*_):
        return jax.tree.map(lambda leaf: jnp.zeros(leaf.shape, leaf.dtype), shapes)

    return lax.cond(index >= 0, steps, nothing, *operands)


def near_first(pair, core):
    return jnp.where(core == 0, pair, pair[::-1])


def on_device(tokens, weight, cotangent, levels):
    token_rows, local_features = tokens.shape
    local_cols = weight.shape[1]
    half = local_features // 2
    dp_count = lax.axis_size("dp")
    dp = lax.axis_index("dp")
    core = dp % 2
    x = dp // (2 * RING)
    tensor = lax.axis_index("tensor")
    wide = jnp.float32
    narrow = jnp.bfloat16

    col_start = tensor * local_cols
    column_ids = col_start + jnp.arange(local_cols, dtype=jnp.int32)
    block_ids = column_ids // BLOCK
    block_range = jnp.arange(levels.shape[0], dtype=jnp.int32)
    membership = (block_ids[None, :] == block_range[:, None]).astype(wide)
    level_vals = levels.astype(wide) / 8.0
    col_scale = jnp.sum(membership * level_vals[:, None], axis=0)

    scaled = (cotangent.astype(wide) * col_scale[None, :]).astype(narrow)
    both = ("dp", "tensor")
    scaled_pair = jnp.concatenate([scaled, from_core(scaled)], axis=0)

    crossed = swap(tokens)
    parts = jnp.stack([crossed[:, :half], crossed[:, half:]])
    parts = jnp.broadcast_to(parts[None], (RING, 2, token_rows, half))
    line = exchange(parts.reshape(2 * RING, token_rows, half), both, groups_core_low())
    line = line.reshape(RING, 2, token_rows, half)
    line = jnp.concatenate([line[i] for i in range(RING)], axis=2)
    line = near_first(line, core)
    line, weight, scaled_pair = lax.optimization_barrier((line, weight, scaled_pair))
    brick = collect(line, "tensor", groups_y()).reshape(-1, RING * half)

    scaled_all = lax.all_gather(scaled_pair, "dp", axis=0, axis_index_groups=groups_x(), tiled=True)

    weight_line = lax.all_gather(weight, "dp", axis=0, axis_index_groups=groups_z(), tiled=True)
    brick, weight_line = lax.optimization_barrier((brick, weight_line))

    grads = lax.dot_general(brick, scaled_all, (((0,), (0,)), ((), ())), preferred_element_type=wide)
    grads = grads.astype(narrow)
    grads, brick, weight_line = lax.optimization_barrier((grads, brick, weight_line))
    grads = lax.psum_scatter(
        grads, "dp", scatter_dimension=0, axis_index_groups=groups_z(), tiled=True
    )
    grad_factor = 1.0 / jnp.sqrt(jnp.float32(token_rows * dp_count))
    weight_grad = grads.astype(wide) * grad_factor

    def sums(scaled_all, brick, weight_line):
        term = lax.dot_general(scaled_all, weight_line, (((1,), (1,)), ((), ())), preferred_element_type=wide)
        term = row_major(term.astype(narrow)).reshape(RING, 2, token_rows, RING * half)
        term = near_first(total(exchange(term, "tensor", groups_y())).astype(narrow), core)
        term = jnp.stack([term[:, :, i * half:(i + 1) * half] for i in range(RING)])

        share = jnp.dot(brick, weight_line, preferred_element_type=wide)
        share = share.reshape(RING, 2, token_rows, local_cols)
        other = from_core(share[:, 1].astype(narrow))
        pieces = []
        for i in range(RING):
            at = (x + i) % RING
            piece = lax.dynamic_index_in_dim(share[:, 0], at, 0, keepdims=False)
            pieces.append(piece + lax.dynamic_index_in_dim(other, at, 0, keepdims=False).astype(wide))
        near = pieces[0]
        away = [piece.astype(narrow) for piece in pieces[1:]]
        running = near
        for i in range(1, RING):
            running += from_x(away[i - 1], -i).astype(wide)

        running, term = lax.optimization_barrier((running, term))
        term = swap(term.reshape(2 * RING, token_rows, half))
        term = exchange(term, both, groups_core_low())
        term = total(term.reshape(RING, 2, token_rows, half)).astype(narrow)
        input_grad = jnp.concatenate([term[0], term[1]], axis=1)
        return running, input_grad

    running, input_grad = block_of(sums, dp, scaled_all, brick, weight_line)
    output = (running * col_scale[None, :]).astype(narrow)
    return (output, input_grad, weight_grad)


def solution(mesh):
    placed = (P("dp", "tensor"), P("dp", "tensor"), P("dp", "tensor"), P())
    return jax.shard_map(
        on_device,
        mesh=mesh,
        in_specs=placed,
        out_specs=(P("dp", "tensor"), P("dp", "tensor"), P("dp", "tensor")),
        check_vma=False,
    )
```

```python
import jax
import jax.numpy as jnp
from jax import lax
from jax.experimental.layout import Layout, with_layout_constraint
from jax.sharding import PartitionSpec as P

BLOCK = 512
RING = 4
GROUPS = 16


def dp_of(x, z, core):
    return ((x % RING) * RING + z % RING) * 2 + core


def swap_pairs():
    return [
        (
            dp_of(y, z, core) * GROUPS + x * RING + low,
            dp_of(x, z, core) * GROUPS + y * RING + low,
        )
        for x in range(RING)
        for z in range(RING)
        for core in range(2)
        for y in range(RING)
        for low in range(RING)
    ]


def dp_pairs(dx, flip):
    return [
        (dp_of(x + dx, z, core ^ flip), dp_of(x, z, core))
        for x in range(RING)
        for z in range(RING)
        for core in range(2)
    ]


def groups_x():
    return [[dp_of(x, z, core) for x in range(RING)] for z in range(RING) for core in range(2)]


def groups_z():
    return [[dp_of(x, z, core) for z in range(RING)] for x in range(RING) for core in range(2)]


def groups_y():
    return [[y * RING + low for y in range(RING)] for low in range(RING)]


def groups_core_low():
    return [
        [
            dp_of(x, z, core) * GROUPS + y * RING + low
            for low in range(RING)
            for core in range(2)
        ]
        for x in range(RING)
        for z in range(RING)
        for y in range(RING)
    ]


def from_core(block):
    return lax.ppermute(block, "dp", dp_pairs(0, 1))


def from_x(block, shift):
    return lax.ppermute(block, "dp", dp_pairs(shift, 0))


def swap(block):
    return lax.ppermute(block, ("dp", "tensor"), swap_pairs())


def row_major(array):
    return with_layout_constraint(array, Layout(major_to_minor=tuple(range(array.ndim))))


def exchange(parts, axis, groups):
    parts = row_major(parts)
    return row_major(lax.all_to_all(parts, axis, 0, 0, axis_index_groups=groups, tiled=True))


def collect(block, axis, groups):
    return exchange(jnp.broadcast_to(block[None], (len(groups[0]),) + block.shape), axis, groups)


def total(parts):
    return jnp.sum(parts.astype(jnp.float32), axis=0)


def block_of(steps, index, *operands):
    shapes = jax.eval_shape(steps, *operands)

    def nothing(*_):
        return jax.tree.map(lambda leaf: jnp.zeros(leaf.shape, leaf.dtype), shapes)

    return lax.cond(index >= 0, steps, nothing, *operands)


def near_first(pair, core):
    return jnp.where(core == 0, pair, pair[::-1])


def on_device(tokens, weight, cotangent, levels):
    token_rows, local_features = tokens.shape
    local_cols = weight.shape[1]
    half = local_features // 2
    dp_count = lax.axis_size("dp")
    dp = lax.axis_index("dp")
    core = dp % 2
    x = dp // (2 * RING)
    tensor = lax.axis_index("tensor")
    wide = jnp.float32
    narrow = jnp.bfloat16

    col_start = tensor * local_cols
    column_ids = col_start + jnp.arange(local_cols, dtype=jnp.int32)
    block_ids = column_ids // BLOCK
    block_range = jnp.arange(levels.shape[0], dtype=jnp.int32)
    membership = (block_ids[None, :] == block_range[:, None]).astype(wide)
    level_vals = levels.astype(wide) / 8.0
    col_scale = jnp.sum(membership * level_vals[:, None], axis=0)

    scaled = (cotangent.astype(wide) * col_scale[None, :]).astype(narrow)
    both = ("dp", "tensor")
    scaled_pair = jnp.concatenate([scaled, from_core(scaled)], axis=0)

    crossed = swap(tokens)
    parts = jnp.stack([crossed[:, :half], crossed[:, half:]])
    parts = jnp.broadcast_to(parts[None], (RING, 2, token_rows, half))
    line = exchange(parts.reshape(2 * RING, token_rows, half), both, groups_core_low())
    line = line.reshape(RING, 2, token_rows, half)
    line = jnp.concatenate([line[i] for i in range(RING)], axis=2)
    line = near_first(line, core)
    line, weight, scaled_pair = lax.optimization_barrier((line, weight, scaled_pair))
    brick = collect(line, "tensor", groups_y()).reshape(-1, RING * half)

    scaled_all = lax.all_gather(scaled_pair, "dp", axis=0, axis_index_groups=groups_x(), tiled=True)

    weight_line = lax.all_gather(weight, "dp", axis=0, axis_index_groups=groups_z(), tiled=True)
    brick, weight_line = lax.optimization_barrier((brick, weight_line))

    grads = lax.dot_general(brick, scaled_all, (((0,), (0,)), ((), ())), preferred_element_type=wide)
    grads = grads.astype(narrow)
    grads, brick, weight_line = lax.optimization_barrier((grads, brick, weight_line))
    grads = lax.psum_scatter(
        grads, "dp", scatter_dimension=0, axis_index_groups=groups_z(), tiled=True
    )
    grad_factor = 1.0 / jnp.sqrt(jnp.float32(token_rows * dp_count))
    weight_grad = grads.astype(wide) * grad_factor

    def sums(scaled_all, brick, weight_line):
        term = lax.dot_general(scaled_all, weight_line, (((1,), (1,)), ((), ())), preferred_element_type=wide)
        term = row_major(term.astype(narrow)).reshape(RING, 2, token_rows, RING * half)
        term = near_first(total(exchange(term, "tensor", groups_y())).astype(narrow), core)
        term = jnp.stack([term[:, :, i * half:(i + 1) * half] for i in range(RING)])

        share = jnp.dot(brick, weight_line, preferred_element_type=wide)
        share = share.reshape(RING, 2, token_rows, local_cols)
        other = from_core(share[:, 1].astype(narrow))
        pieces = []
        for i in range(RING):
            at = (x + i) % RING
            piece = lax.dynamic_index_in_dim(share[:, 0], at, 0, keepdims=False)
            pieces.append(piece + lax.dynamic_index_in_dim(other, at, 0, keepdims=False).astype(wide))
        near = pieces[0]
        away = [piece.astype(narrow) for piece in pieces[1:]]
        away, term = lax.optimization_barrier((away, term))
        running = near
        for i in range(1, RING):
            running += from_x(away[i - 1], -i).astype(wide)

        term = exchange(term.reshape(2 * RING, token_rows, half), both, groups_core_low())
        term = total(term.reshape(RING, 2, token_rows, half)).astype(narrow)
        term = jnp.concatenate([term[0], term[1]], axis=1)
        return running, term

    running, term = block_of(sums, dp, scaled_all, brick, weight_line)
    input_grad = swap(term)
    output = (running * col_scale[None, :]).astype(narrow)
    return (output, input_grad, weight_grad)


def solution(mesh):
    placed = (P("dp", "tensor"), P("dp", "tensor"), P("dp", "tensor"), P())
    return jax.shard_map(
        on_device,
        mesh=mesh,
        in_specs=placed,
        out_specs=(P("dp", "tensor"), P("dp", "tensor"), P("dp", "tensor")),
        check_vma=False,
    )
```
